256 devices in a mesh: ctx: 64 (over y, z, core), head: 4 (over x).
Axes of the slice: x: 4, y: 4, z: 8, core: 2. Of those that a mesh axis runs over, the one named last changes fastest.
Arguments:
- queries: bfloat16 [32768, 2048], P('ctx', 'head'), may hold values from -6 to 6
- keys: bfloat16 [32768, 2048], P('ctx', 'head'), may hold values from -6 to 6
- values: bfloat16 [32768, 2048], P('ctx', 'head'), may hold values from -6 to 6
- gain: bfloat16 [2048], P('head'), may hold values from 0.099609375 to 1.8984375
- out_weight: bfloat16 [2048, 4096], P('head', 'ctx'), may hold values from -0.125 to 0.125
- cotangent: bfloat16 [32768, 4096], P('ctx', 'head'), may hold values from -16 to 16
Outputs:
- layer_out: bfloat16 [32768, 4096], P('ctx', 'head')
- grad_queries: bfloat16 [32768, 2048], P('ctx', 'head')
- grad_keys: bfloat16 [32768, 2048], P('ctx', 'head')
- grad_values: bfloat16 [32768, 2048], P('ctx', 'head')
- grad_out_weight: float32 [2048, 4096], P('head', 'ctx')
The draws below stay inside these ranges and needn't reach their ends.
All inputs are finite; a program needn't handle non-finite values.
Results may differ from the reference program's by a relative error of at most 0.02.
Values may be sent and summed in bfloat16 or wider, within the bound.
A program may use at most 128 MiB of HBM per device.

```python
import jax
import jax.numpy as jnp
from jax import lax

D = 4096
HEADS = 16
HDIM = 128
BLOCK = 512
TOKENS = 32768
HD = 2048


def strengthened(values, key, source, target, blocks, factor):
    owner, partner = [(jnp.arange(values.shape[axis_at]) // (values.shape[axis_at] // blocks)).reshape([-1 if axis == axis_at else 1 for axis in range(values.ndim)]) for axis_at in (source, target)]
    chosen = jax.random.permutation(key, blocks)[partner]
    strong = (owner == chosen) | (owner == (partner + blocks // 2) % blocks)
    return jnp.where(strong, factor * values, values)


def level_of(own_key, extent, pieces, low, high):
    factor_of = 1.0
    for dim, parts in pieces:
        heights = jax.random.uniform(jax.random.fold_in(jax.random.fold_in(own_key, 6), dim), (parts,), jnp.float32, low / len(pieces), high / len(pieces))
        factor_of = factor_of * jnp.repeat(jnp.exp(heights), extent[dim] // parts).reshape((-1,) + (1,) * (len(extent) - 1 - dim))
    return factor_of


def normal_values(own_key, extent, width, bound, shards=(), kind=jnp.bfloat16):
    values = width * jax.random.normal(own_key, extent, jnp.float32)
    if shards:
        values = values * level_of(own_key, extent, shards, -0.22, 0.18)
    return jnp.clip(values, -bound, bound).astype(kind)


def bell_draw_with(stream_key, shape, width, most, shards, heavy, held_as=jnp.bfloat16):
    values = width * jax.random.normal(stream_key, shape, jnp.float32)
    if shards:
        values = values * level_of(stream_key, shape, shards, -0.22, 0.18)
    return jnp.clip(strengthened(values, jax.random.fold_in(stream_key, 3), *heavy), -most, most).astype(held_as)


def setup_inputs(seed: int = 0) -> dict:
    key_of = jax.random.split(jax.random.key(seed), 7)
    return {
        "queries": normal_values(key_of[0], (TOKENS, HD), 1.0, 6.0, ((0, 64), (1, 4))),
        "keys": normal_values(key_of[1], (TOKENS, HD), 1.0, 6.0, ((0, 64), (1, 4))),
        "values": normal_values(key_of[2], (TOKENS, HD), 1.0, 6.0, ((0, 64), (1, 4))),
        "gain": jnp.clip(1.0 + 0.18 * jax.random.normal(key_of[3], (HD,), jnp.float32), 0.099609375, 1.8984375).astype(jnp.bfloat16),
        "out_weight": normal_values(key_of[4], (HD, D), HD ** -0.5, 0.125, ((0, 4), (1, 64))),
        "cotangent": bell_draw_with(key_of[5], (TOKENS, D), 1.0, 16.0, ((0, 64), (1, 4)), (0, 1, 64, 4.0)),
    }


EPS = 1e-06

def rounded(x):
    return lax.optimization_barrier(x.astype(jnp.bfloat16)).astype(jnp.float32)

def block_lookup(array, block_index):
    start = (block_index * BLOCK).astype(jnp.int32)
    return lax.dynamic_slice_in_dim(array, start, BLOCK, 0).reshape(BLOCK, HEADS, HDIM).astype(jnp.float32)

def reference(queries, keys, values, gain, out_weight, cotangent):
    blocks = TOKENS // BLOCK
    order = jnp.arange(blocks, dtype=jnp.int32)
    causal = jnp.arange(BLOCK)[:, None] >= jnp.arange(BLOCK)[None, :]
    gains = gain.astype(jnp.float32).reshape(HEADS, HDIM)
    zero = jnp.zeros((1, HEADS, HDIM, HDIM), jnp.float32)

    def state_of(block_index):
        return jnp.einsum('api,apr->pir', block_lookup(keys, block_index), block_lookup(values, block_index))
    states = lax.map(state_of, order)
    prefix_state = rounded(jnp.concatenate([zero, jnp.cumsum(states, axis=0)[:-1]], axis=0))

    def mixing_of(block_index):
        query_rows = block_lookup(queries, block_index)
        scores = jnp.einsum('bhk,chk->hbc', query_rows, block_lookup(keys, block_index))
        return rounded(jnp.where(causal, scores, 0.0))

    def attend(block_index):
        mixing_matrix = mixing_of(block_index)
        attended_rows = jnp.einsum('hbc,chv->bhv', mixing_matrix, block_lookup(values, block_index))
        attended_rows = attended_rows + jnp.einsum('nrt,rts->nrs', block_lookup(queries, block_index), prefix_state[block_index])
        scale = lax.rsqrt(lax.optimization_barrier(jnp.mean(attended_rows * attended_rows, axis=-1, keepdims=True)) + EPS)
        return (attended_rows, scale)

    def forward(block_index):
        attended_rows, scale = attend(block_index)
        normed = (attended_rows * scale * gains).astype(jnp.bfloat16).reshape(BLOCK, HD)
        output = jnp.dot(normed, out_weight, preferred_element_type=jnp.float32).astype(jnp.bfloat16)
        return (normed, output)
    normed, layer_out = lax.map(forward, order)
    normed = normed.reshape(TOKENS, HD)
    layer_out = layer_out.reshape(TOKENS, D)

    def backward(block_index):
        attended_rows, scale = attend(block_index)
        start = (block_index * BLOCK).astype(jnp.int32)
        cot = lax.dynamic_slice_in_dim(cotangent, start, BLOCK, 0)
        grad_normed = jnp.dot(cot, out_weight.T, preferred_element_type=jnp.float32).reshape(BLOCK, HEADS, HDIM)
        weighted = grad_normed * gains
        along = lax.optimization_barrier(jnp.mean(weighted * attended_rows, axis=-1, keepdims=True))
        attention_gradient = (scale * weighted - scale * scale * scale * attended_rows * along).astype(jnp.bfloat16)
        state_gradient = jnp.einsum('api,apr->pir', block_lookup(queries, block_index), attention_gradient.astype(jnp.float32))
        return (attention_gradient, state_gradient)
    grad_atts, grad_states = lax.map(backward, order)
    inclusive = jnp.flip(jnp.cumsum(jnp.flip(grad_states, 0), axis=0), 0)
    suffix_state = rounded(jnp.concatenate([inclusive[1:], zero], axis=0))

    def gradients(block_index):
        query_rows = block_lookup(queries, block_index)
        key = block_lookup(keys, block_index)
        value_rows = block_lookup(values, block_index)
        mixing_matrix = mixing_of(block_index)
        attention_gradient = grad_atts[block_index].astype(jnp.float32)
        mixing_gradient = rounded(jnp.where(causal, jnp.einsum('bhv,chv->hbc', attention_gradient, value_rows), 0.0))
        query_gradient = jnp.einsum('tpg,gtx->ptx', mixing_gradient, key) + jnp.einsum('lyw,yrw->lyr', attention_gradient, prefix_state[block_index])
        key_gradient = jnp.einsum('auj,uap->jap', mixing_gradient, query_rows) + jnp.einsum('lym,yam->lya', value_rows, suffix_state[block_index])
        value_gradient = jnp.einsum('jft,fjm->tjm', mixing_matrix, attention_gradient) + jnp.einsum('eux,uxm->eum', key, suffix_state[block_index])
        return (query_gradient.astype(jnp.bfloat16).reshape(BLOCK, HD), key_gradient.astype(jnp.bfloat16).reshape(BLOCK, HD), value_gradient.astype(jnp.bfloat16).reshape(BLOCK, HD))
    grad_queries, grad_keys, grad_values = lax.map(gradients, order)
    grad_out_weight = jnp.dot(normed.T, cotangent, preferred_element_type=jnp.float32)
    return (layer_out, grad_queries.reshape(TOKENS, HD), grad_keys.reshape(TOKENS, HD), grad_values.reshape(TOKENS, HD), grad_out_weight)
```

```python
import jax
import jax.numpy as jnp
from jax import lax
from jax.experimental import pallas as pl
from jax.experimental.pallas import tpu as pltpu
from jax.sharding import PartitionSpec as P

HDIM = 128
HEADS = 4
ROWS = 512
NX, NY, NZ = 4, 4, 8
GROUP = 2 * NZ
SLICE = HEADS * HDIM // GROUP
PIECE = 64
EPS = 1e-06
MESH = pl.DeviceIdType.MESH
F32, BF16 = jnp.float32, jnp.bfloat16


def dot(a, b, ca, cb):
    return lax.dot_general(a, b, (((ca,), (cb,)), ((), ())), preferred_element_type=F32)


def copy_to(src, dst, send_sem, recv_sem, device):
    return pltpu.make_async_remote_copy(
        src_ref=src, dst_ref=dst, send_sem=send_sem, recv_sem=recv_sem,
        device_id=device, device_id_type=MESH,
    )


def head(h):
    return slice(h * HDIM, (h + 1) * HDIM)


def kernel(
    q_ref, k_ref, v_ref, g_ref, w_ref, c_ref,
    out_ref, gq_ref, gk_ref, gv_ref, gw_ref,
    wt, state, slices, partial, totals, back, states,
    att, inv, normed, cot_t, gn_stage, gn_recv, gn_own, ga,
    pair_stage, pair_recv, dsum, ring_stage, ring_recv, last_stage, last_recv,
    w0_send, w0_recv, wz_send, wz_recv, wc_send, wc_recv,
    s1_send, s1_recv, s2_send, s2_recv, s3_send, s3_recv,
    n_send, n_recv, gn_send, gn_rsem, pair_send, pair_rsem,
    ring_send, ring_rsem, last_send, last_rsem,
):
    ctx, x = lax.axis_index("ctx"), lax.axis_index("head")
    y, z, core = ctx // GROUP, (ctx // 2) % NZ, ctx % 2
    g = ctx % GROUP
    me_diag = x == y

    def dev(x, y, z, core):
        return (y * GROUP + z * 2 + core, x)

    step = 1 - 2 * core
    z_major, z_minor = (z + step + NZ) % NZ, (z - step + NZ) % NZ
    x_major, x_minor, x_opp = (x + step + NX) % NX, (x - step + NX) % NX, (x + 2) % NX
    d_major, d_minor = dev(x, y, z_major, core), dev(x, y, z_minor, core)
    e_major, e_minor = dev(x_major, y, z, core), dev(x_minor, y, z, core)
    sibling = dev(x, y, z, 1 - core)
    sent = []

    def send(*args):
        c = copy_to(*args)
        c.start()
        sent.append(c)

    barrier = pltpu.get_barrier_semaphore()

    def hello(device):
        pl.semaphore_signal(barrier, inc=1, device_id=device, device_id_type=MESH)

    def hello_group(d, carry):
        hello((y * GROUP + (g + d) % GROUP, x))
        return carry

    lax.fori_loop(1, GROUP, hello_group, 0)
    for d in range(1, NY):
        hello(dev(x, (y + d) % NY, z, core))
    hello(e_major)
    hello(e_minor)
    for j in range(NX):
        for there in ((y, j), (j, x)):
            @pl.when(jnp.logical_or(there[0] != x, there[1] != y))
            def _():
                hello(dev(there[0], there[1], z, core))
    pl.semaphore_wait(barrier, (GROUP - 1) + (NY - 1) + 2 + 2 * NX - 2 * me_diag.astype(jnp.int32))

    for j in range(NY):
        away = jnp.logical_or(y != x, j != y)

        @pl.when(away)
        def _():
            copy_to(w_ref, wt.at[z, core, x], w0_send.at[j], w0_recv.at[x], dev(y, j, z, core)).start()

        @pl.when(jnp.logical_not(away))
        def _():
            wt[z, core, x] = w_ref[...]

    def scan_start(way):
        for h in range(HEADS):
            state[way, h * (HDIM // SLICE):(h + 1) * (HDIM // SLICE)] = (
                scan_term(way, h).astype(BF16).reshape(HDIM // SLICE, SLICE, HDIM)
            )

        def go(d, carry):
            to = (g + d) % GROUP
            copy_to(state.at[way, to], slices.at[way, g], s1_send.at[way, d], s1_recv.at[way, g],
                    (y * GROUP + to, x)).start()
            return carry

        lax.fori_loop(1, GROUP, go, 0)
        slices[way, g] = state[way, g]

    def scan_term(way, h):
        if way == 0:
            return dot(k_ref[:, head(h)], v_ref[:, head(h)], 0, 0)
        return dot(q_ref[:, head(h)], ga[:, head(h)], 0, 0)

    def scan_totals(way):
        def arrive(d, carry):
            at = (g + d) % GROUP
            copy_to(slices.at[way, at], slices.at[way, at], s1_send.at[way, d], s1_recv.at[way, at], sibling).wait_recv()
            return carry

        lax.fori_loop(1, GROUP, arrive, 0)
        run = jnp.zeros((SLICE, HDIM), F32)
        for i in (range(GROUP) if way == 0 else range(GROUP - 1, -1, -1)):
            partial[way, i] = run
            run = run + slices[way, i].astype(F32)
        totals[way, y] = run
        for d in range(1, NY):
            send(totals.at[way, y], totals.at[way, y], s2_send.at[way, d], s2_recv.at[way, y],
                 dev(x, (y + d) % NY, z, core))

    def scan_back(way):
        for d in range(1, NY):
            at = (y + d) % NY
            copy_to(totals.at[way, at], totals.at[way, at], s2_send.at[way, d], s2_recv.at[way, at], sibling).wait_recv()
        offset = jnp.zeros((SLICE, HDIM), F32)
        for j in range(NY):
            counts = (j < y) if way == 0 else (j > y)
            offset = offset + jnp.where(counts, totals[way, j], 0.0)
        for i in range(GROUP):
            back[way, i] = (partial[way, i] + offset).astype(BF16)

        def go(d, carry):
            to = (g + d) % GROUP
            copy_to(back.at[way, to], states.at[way, g], s3_send.at[way, d], s3_recv.at[way, g],
                    (y * GROUP + to, x)).start()
            return carry

        lax.fori_loop(1, GROUP, go, 0)
        states[way, g] = back[way, g]

    def scan_end(way):
        def arrive(d, carry):
            at = (g + d) % GROUP
            copy_to(states.at[way, at], states.at[way, at], s3_send.at[way, d], s3_recv.at[way, at], sibling).wait_recv()
            return carry

        lax.fori_loop(1, GROUP, arrive, 0)

    def state_of(way, h):
        n = HDIM // SLICE
        return states[way, h * n:(h + 1) * n].reshape(HDIM, HDIM)

    scan_start(0)

    def to_sibling(i, at):
        send(wt.at[at, core], wt.at[at, core], wc_send.at[i], wc_recv.at[i], sibling)

    def w_first():
        for a in range(NX):
            @pl.when(jnp.logical_or(y != x, a != x))
            def _():
                copy_to(wt.at[z, core, a], wt.at[z, core, a], w0_send.at[a], w0_recv.at[a], sibling).wait_recv()
        send(wt.at[z, core], wt.at[z, core], wz_send.at[0], wz_recv.at[0], d_major)
        send(wt.at[z, core], wt.at[z, core], wz_send.at[4], wz_recv.at[4], d_minor)
        to_sibling(0, z)

    def w_wait(i, at):
        copy_to(wt.at[at, core], wt.at[at, core], wz_send.at[i], wz_recv.at[i], sibling).wait_recv()

    def w_step(s):
        at = (z - step * s + NZ) % NZ
        w_wait(s - 1, at)
        if s < 4:
            send(wt.at[at, core], wt.at[at, core], wz_send.at[s], wz_recv.at[s], d_major)
        to_sibling(s, at)
        if s < 4:
            at = (z + step * s + NZ) % NZ
            w_wait(3 + s, at)
            if s < 3:
                send(wt.at[at, core], wt.at[at, core], wz_send.at[4 + s], wz_recv.at[4 + s], d_minor)
            to_sibling(4 + s, at)

    def w_end():
        for s in range(8):
            at = (z - step * (s - 4) + NZ) % NZ if s > 4 else (z + step * s + NZ) % NZ
            copy_to(wt.at[at, 1 - core], wt.at[at, 1 - core], wc_send.at[s], wc_recv.at[s], sibling).wait_recv()

    row = lax.broadcasted_iota(jnp.int32, (ROWS, ROWS), 0)
    col = lax.broadcasted_iota(jnp.int32, (ROWS, ROWS), 1)

    def local_attention(h):
        s = dot(q_ref[:, head(h)], k_ref[:, head(h)], 1, 1)
        m = jnp.where(row >= col, s, 0.0).astype(BF16)
        att[:, head(h)] = dot(m, v_ref[:, head(h)], 1, 0)

    w_first()
    local_attention(0)
    local_attention(1)
    scan_totals(0)
    w_step(1)
    local_attention(2)
    local_attention(3)
    scan_back(0)
    w_step(2)
    cot_t[...] = c_ref[...].T.reshape(NZ, 2, PIECE, ROWS)
    scan_end(0)

    gain = g_ref[...].astype(F32)
    for h in range(HEADS):
        a = att[:, head(h)] + dot(q_ref[:, head(h)], state_of(0, h), 1, 0)
        scale = lax.rsqrt(jnp.mean(a * a, axis=-1, keepdims=True) + EPS)
        a = a * scale
        att[:, head(h)] = a
        inv[h] = scale
        normed[x, :, head(h)] = (a * gain[:, head(h)]).astype(BF16)
    send(normed.at[x], normed.at[x], n_send.at[0], n_recv.at[0], e_major)
    send(normed.at[x], normed.at[x], n_send.at[1], n_recv.at[1], e_minor)
    w_step(3)

    def n_wait(i, at):
        copy_to(normed.at[at], normed.at[at], n_send.at[i], n_recv.at[i], sibling).wait_recv()

    def pair_go(p, a):
        other = cot_t[:, 1 - core].reshape(ROWS, ROWS)
        pair_stage[p] = dot(other, normed[a], 1, 0).astype(BF16).reshape(NZ, PIECE, ROWS)
        send(pair_stage.at[p], pair_recv.at[p], pair_send.at[p], pair_rsem.at[p], sibling)
        mine = cot_t[:, core].reshape(ROWS, ROWS)
        dsum[p] = dot(mine, normed[a], 1, 0).reshape(NZ, PIECE, ROWS)

    def pair_end(p):
        copy_to(pair_stage.at[p], pair_recv.at[p], pair_send.at[p], pair_rsem.at[p], sibling).wait_recv()
        dsum[p] = dsum[p] + pair_recv[p].astype(F32)

    def ring_wait(p, i):
        copy_to(ring_stage.at[p, i], ring_recv.at[p, i], ring_send.at[p, i], ring_rsem.at[p, i], sibling).wait_recv()

    def ring_step(p, s):
        at = (z + step * (4 - s) + NZ) % NZ
        term = dsum[p, at]
        if s:
            ring_wait(p, s - 1)
            term = term + ring_recv[p, s - 1].astype(F32)
        ring_stage[p, s] = term.astype(BF16)
        send(ring_stage.at[p, s], ring_recv.at[p, s], ring_send.at[p, s], ring_rsem.at[p, s], d_major)
        if s < 3:
            at = (z - step * (3 - s) + NZ) % NZ
            term = dsum[p, at]
            if s:
                ring_wait(p, 3 + s)
                term = term + ring_recv[p, 3 + s].astype(F32)
            i = 4 + s
            ring_stage[p, i] = term.astype(BF16)
            send(ring_stage.at[p, i], ring_recv.at[p, i], ring_send.at[p, i], ring_rsem.at[p, i], d_minor)

    def ring_end(p, a):
        ring_wait(p, 3)
        ring_wait(p, 6)
        total = dsum[p, z] + ring_recv[p, 3].astype(F32) + ring_recv[p, 6].astype(F32)
        last_stage[p] = total.astype(BF16)
        away = jnp.logical_or(a != x, x != y)

        @pl.when(away)
        def _():
            copy_to(last_stage.at[p], last_recv.at[y], last_send.at[p], last_rsem.at[y], dev(a, x, z, core)).start()

        @pl.when(jnp.logical_not(away))
        def _():
            last_recv[y] = last_stage[p]

    quarters = (x, (x + 3) % NX, (x + 1) % NX, x_opp)

    def ring_all(p):
        pair_end(p)
        for s in range(4):
            ring_step(p, s)

    def gn_part(a):
        w = wt[:, :, a].reshape(NZ * 2 * PIECE, ROWS)
        return dot(c_ref[...], w, 1, 0)

    def gn_wait(i):
        copy_to(gn_stage.at[i], gn_recv.at[i], gn_send.at[i], gn_rsem.at[i], sibling).wait_recv()

    pair_go(0, quarters[0])
    w_step(4)
    w_end()
    gn_stage[0] = gn_part(x_opp).astype(BF16)
    send(gn_stage.at[0], gn_recv.at[0], gn_send.at[0], gn_rsem.at[0], e_major)
    n_wait(0, x_minor)
    send(normed.at[x_minor], normed.at[x_minor], n_send.at[2], n_recv.at[2], e_major)
    gn_stage[1] = gn_part(x_minor).astype(BF16)
    send(gn_stage.at[1], gn_recv.at[1], gn_send.at[1], gn_rsem.at[1], e_minor)
    ring_all(0)
    n_wait(1, x_major)
    pair_go(1, quarters[1])
    pair_go(2, quarters[2])
    gn_wait(0)
    gn_stage[2] = (gn_part(x_major) + gn_recv[0].astype(F32)).astype(BF16)
    send(gn_stage.at[2], gn_recv.at[2], gn_send.at[2], gn_rsem.at[2], e_major)
    gn_own[...] = gn_part(x)
    pair_end(1)
    pair_end(2)
    for s in range(4):
        ring_step(1, s)
        ring_step(2, s)
    n_wait(2, x_opp)
    pair_go(3, quarters[3])
    ring_all(3)
    for p in range(3):
        ring_end(p, quarters[p])

    gn_wait(1)
    gn_wait(2)
    for h in range(HEADS):
        w = gn_own[:, head(h)] + gn_recv[1, :, head(h)].astype(F32) + gn_recv[2, :, head(h)].astype(F32)
        w = w * gain[:, head(h)]
        a = att[:, head(h)]
        along = jnp.mean(w * a, axis=-1, keepdims=True)
        ga[:, head(h)] = (inv[h] * (w - a * along)).astype(BF16)
    scan_start(1)
    ring_end(3, quarters[3])

    def queries_gradient(h):
        s = dot(ga[:, head(h)], v_ref[:, head(h)], 1, 1)
        m = jnp.where(row >= col, s, 0.0).astype(BF16)
        t = dot(m, k_ref[:, head(h)], 1, 0) + dot(ga[:, head(h)], state_of(0, h), 1, 1)
        gq_ref[:, head(h)] = t.astype(BF16)

    def local_keys_values(h):
        s = dot(v_ref[:, head(h)], ga[:, head(h)], 1, 1)
        m = jnp.where(col >= row, s, 0.0).astype(BF16)
        gn_own[:, head(h)] = dot(m, q_ref[:, head(h)], 1, 0)
        s = dot(k_ref[:, head(h)], q_ref[:, head(h)], 1, 1)
        m = jnp.where(col >= row, s, 0.0).astype(BF16)
        att[:, head(h)] = dot(m, ga[:, head(h)], 1, 0)

    for h in range(HEADS):
        queries_gradient(h)
    scan_totals(1)
    for h in range(HEADS):
        local_keys_values(h)
    scan_back(1)

    def out_rows(i, carry):
        r = pl.ds(pl.multiple_of(i * 128, 128), 128)
        total = jnp.zeros((128, NZ * 2 * PIECE), F32)
        for a in range(NX):
            w = wt[:, :, a].reshape(NZ * 2 * PIECE, ROWS)
            total = total + dot(normed[a, r, :], w, 1, 1)
        out_ref[r, :] = total.astype(BF16)
        return carry

    lax.fori_loop(0, ROWS // 128, out_rows, 0)

    scan_end(1)
    for h in range(HEADS):
        st = state_of(1, h)
        gk_ref[:, head(h)] = (gn_own[:, head(h)] + dot(v_ref[:, head(h)], st, 1, 1)).astype(BF16)
        gv_ref[:, head(h)] = (att[:, head(h)] + dot(k_ref[:, head(h)], st, 1, 0)).astype(BF16)

    for j in range(NY):
        @pl.when(jnp.logical_or(y != x, j != y))
        def _():
            copy_to(last_stage.at[0], last_recv.at[j], last_send.at[0], last_rsem.at[j], sibling).wait_recv()
    gw_ref[...] = (
        (last_recv[0].astype(F32) + last_recv[1].astype(F32))
        + (last_recv[2].astype(F32) + last_recv[3].astype(F32))
    )

    for c in sent:
        c.wait_send()
    for j in range(NY):
        @pl.when(jnp.logical_or(y != x, j != y))
        def _():
            copy_to(w_ref, wt.at[z, core, x], w0_send.at[j], w0_recv.at[x], sibling).wait_send()
    for p in range(NX):
        @pl.when(jnp.logical_or(quarters[p] != x, y != x))
        def _():
            copy_to(last_stage.at[p], last_recv.at[y], last_send.at[p], last_rsem.at[y], sibling).wait_send()

    def left(d, carry):
        for way in range(2):
            to = (g + d) % GROUP
            copy_to(state.at[way, to], slices.at[way, g], s1_send.at[way, d], s1_recv.at[way, g], sibling).wait_send()
            copy_to(back.at[way, to], states.at[way, g], s3_send.at[way, d], s3_recv.at[way, g], sibling).wait_send()
        return carry

    lax.fori_loop(1, GROUP, left, 0)


def on_device(queries, keys, values, gain, out_weight, cotangent):
    width = HEADS * HDIM
    cols = NZ * 2 * PIECE
    vmem = pl.BlockSpec(memory_space=pltpu.VMEM)
    dma = pltpu.SemaphoreType.DMA
    outs = pl.pallas_call(
        kernel,
        out_shape=(
            jax.ShapeDtypeStruct((ROWS, cols), BF16),
            jax.ShapeDtypeStruct((ROWS, width), BF16),
            jax.ShapeDtypeStruct((ROWS, width), BF16),
            jax.ShapeDtypeStruct((ROWS, width), BF16),
            jax.ShapeDtypeStruct((PIECE, width), F32),
        ),
        in_specs=[vmem] * 6,
        out_specs=(vmem,) * 5,
        scratch_shapes=[
            pltpu.VMEM((NZ, 2, NX, PIECE, width), BF16),
            pltpu.VMEM((2, GROUP, SLICE, HDIM), BF16),
            pltpu.VMEM((2, GROUP, SLICE, HDIM), BF16),
            pltpu.VMEM((2, GROUP, SLICE, HDIM), F32),
            pltpu.VMEM((2, NY, SLICE, HDIM), F32),
            pltpu.VMEM((2, GROUP, SLICE, HDIM), BF16),
            pltpu.VMEM((2, GROUP, SLICE, HDIM), BF16),
            pltpu.VMEM((ROWS, width), F32),
            pltpu.VMEM((HEADS, ROWS, 1), F32),
            pltpu.VMEM((NX, ROWS, width), BF16),
            pltpu.VMEM((NZ, 2, PIECE, ROWS), BF16),
            pltpu.VMEM((3, ROWS, width), BF16),
            pltpu.VMEM((3, ROWS, width), BF16),
            pltpu.VMEM((ROWS, width), F32),
            pltpu.VMEM((ROWS, width), BF16),
            pltpu.VMEM((NX, NZ, PIECE, width), BF16),
            pltpu.VMEM((NX, NZ, PIECE, width), BF16),
            pltpu.VMEM((NX, NZ, PIECE, width), F32),
            pltpu.VMEM((NX, 7, PIECE, width), BF16),
            pltpu.VMEM((NX, 7, PIECE, width), BF16),
            pltpu.VMEM((NX, PIECE, width), BF16),
            pltpu.VMEM((NY, PIECE, width), BF16),
            dma((NY,)), dma((NX,)), dma((7,)), dma((7,)), dma((8,)), dma((8,)),
            dma((2, GROUP)), dma((2, GROUP)), dma((2, NY)), dma((2, NY)), dma((2, GROUP)), dma((2, GROUP)),
            dma((3,)), dma((3,)), dma((3,)), dma((3,)), dma((NX,)), dma((NX,)),
            dma((NX, 7)), dma((NX, 7)), dma((NX,)), dma((NY,)),
        ],
        compiler_params=pltpu.CompilerParams(
            collective_id=0, has_side_effects=True, vmem_limit_bytes=56 * 1024 * 1024
        ),
    )(queries, keys, values, gain.reshape(1, width), out_weight.T, cotangent)
    return outs[:4] + (outs[4].T,)


def solution(mesh):
    in_specs = (
        P("ctx", "head"),
        P("ctx", "head"),
        P("ctx", "head"),
        P("head"),
        P("head", "ctx"),
        P("ctx", "head"),
    )
    out_specs = (
        P("ctx", "head"),
        P("ctx", "head"),
        P("ctx", "head"),
        P("ctx", "head"),
        P("head", "ctx"),
    )
    return jax.shard_map(
        on_device, mesh=mesh, in_specs=in_specs, out_specs=out_specs, check_vma=False
    )
```

```python
import jax
import jax.numpy as jnp
from jax import lax
from jax.experimental import pallas as pl
from jax.experimental.pallas import tpu as pltpu
from jax.sharding import PartitionSpec as P

HDIM = 128
HEADS = 4
ROWS = 512
NX, NY, NZ = 4, 4, 8
GROUP = 2 * NZ
SLICE = HEADS * HDIM // GROUP
PIECE = 64
EPS = 1e-06
MESH = pl.DeviceIdType.MESH
F32, BF16 = jnp.float32, jnp.bfloat16


def dot(a, b, ca, cb):
    return lax.dot_general(a, b, (((ca,), (cb,)), ((), ())), preferred_element_type=F32)


def copy_to(src, dst, send_sem, recv_sem, device):
    return pltpu.make_async_remote_copy(
        src_ref=src, dst_ref=dst, send_sem=send_sem, recv_sem=recv_sem,
        device_id=device, device_id_type=MESH,
    )


def head(h):
    return slice(h * HDIM, (h + 1) * HDIM)


class Ring:
    def __init__(self, n, at, step, view, send_sem, recv_sem, device, sent, landed=None):
        self.n, self.at, self.step, self.view = n, at, step, view
        self.sems = send_sem, recv_sem
        self.major, self.minor = device((at + step + n) % n), device((at - step + n) % n)
        self.sent, self.landed = sent, landed

    def send(self, i, src, place, way):
        c = copy_to(src, self.view(place), self.sems[0].at[i], self.sems[1].at[i], way)
        c.start()
        self.sent.append(c)

    def arrive(self, i, place):
        view = self.view(place)
        copy_to(view, view, self.sems[0].at[i], self.sems[1].at[i], self.major).wait_recv()

    def start(self, src=None):
        src = self.view(self.at) if src is None else src
        self.send(0, src, self.at, self.major)
        self.send(self.n // 2, src, self.at, self.minor)
        if self.landed:
            self.landed(self.at)

    def go(self, s):
        n, half = self.n, self.n // 2
        places = [((self.at - self.step * s + n) % n, s - 1, s, self.major, s < half)]
        if s < half:
            places.append(((self.at + self.step * s + n) % n, half + s - 1, half + s, self.minor, s < half - 1))
        for place, came, goes, way, more in places:
            self.arrive(came, place)
            if more:
                self.send(goes, self.view(place), place, way)
            if self.landed:
                self.landed(place)


def kernel(
    q_ref, k_ref, v_ref, g_ref, w_ref, c_ref,
    out_ref, gq_ref, gk_ref, gv_ref, gw_ref,
    wt, wc, ca, state, slices, partial, totals, back, states,
    att, inv, normed, cot_t, gn, ga,
    pair_stage, pair_recv, dsum, ring_stage, ring_recv, last_stage, last_recv,
    ay_send, ay_recv, az_send, az_recv, ac_send, ac_recv,
    bz_send, bz_recv, by_send, by_recv, bc_send, bc_recv,
    pm_send, pm_recv, cz_send, cz_recv, cy_send, cy_recv, cc_send, cc_recv,
    ca_send, ca_recv,
    s1_send, s1_recv, s2_send, s2_recv, s3_send, s3_recv,
    n_send, n_recv, pair_send, pair_rsem,
    ring_send, ring_rsem, last_send, last_rsem,
):
    ctx, x = lax.axis_index("ctx"), lax.axis_index("head")
    y, z, core = ctx // GROUP, (ctx // 2) % NZ, ctx % 2
    g = ctx % GROUP
    me_diag = x == y

    def dev(x, y, z, core):
        return (y * GROUP + z * 2 + core, x)

    step = 1 - 2 * core
    z_major, z_minor = (z + step + NZ) % NZ, (z - step + NZ) % NZ
    x_opp = (x + 2) % NX
    d_major, d_minor = dev(x, y, z_major, core), dev(x, y, z_minor, core)
    sibling = dev(x, y, z, 1 - core)
    sent = []

    def send(*args):
        c = copy_to(*args)
        c.start()
        sent.append(c)

    barrier = pltpu.get_barrier_semaphore()

    def hello(device):
        pl.semaphore_signal(barrier, inc=1, device_id=device, device_id_type=MESH)

    def hello_group(d, carry):
        hello((y * GROUP + (g + d) % GROUP, x))
        return carry

    lax.fori_loop(1, GROUP, hello_group, 0)
    for d in range(1, NY):
        hello(dev(x, (y + d) % NY, z, core))
    hello(dev((x + 1) % NX, y, z, core))
    hello(dev((x + 3) % NX, y, z, core))

    @pl.when(x != y)
    def _():
        hello(dev(y, x, z, core))


    def on_y(j):
        return dev(x, j, z, core)

    def on_z(j):
        return dev(x, y, j, core)

    def on_x(j):
        return dev(j, y, z, core)

    def exchange(view, send_sem, recv_sem):
        def landed(place):
            send(view(place), view(place), send_sem.at[place], recv_sem.at[place], sibling)

        return landed

    def exchanged(n, view, send_sem, recv_sem):
        for i in range(n):
            copy_to(view(i), view(i), send_sem.at[i], recv_sem.at[i], sibling).wait_recv()

    half = PIECE // 2
    low, high = pl.ds(0, half), pl.ds(half, half)
    az_view = lambda i, c=core: wt.at[i, c, :, low]
    by_view = lambda i, c=core: wt.at[:, c, i, high]
    cy_view = lambda i, c=core: wc.at[i, :, c]
    ring_ay = Ring(NY, y, step, lambda i: wt.at[z, core, i, low], ay_send, ay_recv, on_y, sent)
    ring_az = Ring(NZ, z, step, az_view, az_send, az_recv, on_z, sent, exchange(az_view, ac_send, ac_recv))
    ring_bz = Ring(NZ, z, step, lambda i: wt.at[i, core, y, high], bz_send, bz_recv, on_z, sent)
    ring_by = Ring(NY, y, step, by_view, by_send, by_recv, on_y, sent, exchange(by_view, bc_send, bc_recv))
    ring_cz = Ring(NZ, z, step, lambda i: wc.at[y, i, core], cz_send, cz_recv, on_z, sent)
    ring_cy = Ring(NY, y, step, cy_view, cy_send, cy_recv, on_y, sent, exchange(cy_view, cc_send, cc_recv))
    rows = [pl.ds(0, ROWS // 2), pl.ds(ROWS // 2, ROWS // 2)]
    ring_cot = [
        Ring(NX, x, step, lambda i, r=r: ca.at[i, r], ca_send.at[h], ca_recv.at[h], on_x, sent)
        for h, r in enumerate(rows)
    ]
    ring_n = Ring(NX, x, step, lambda i: normed.at[i], n_send, n_recv, on_x, sent)

    def turned():
        @pl.when(x != y)
        def _():
            copy_to(w_ref, wc.at[y, z, core], pm_send.at[0], pm_recv.at[0], sibling).wait_recv()

    def scan_state(way):
        for h in range(HEADS):
            state[way, h * (HDIM // SLICE):(h + 1) * (HDIM // SLICE)] = (
                scan_term(way, h).astype(BF16).reshape(HDIM // SLICE, SLICE, HDIM)
            )

    def scan_start(way):
        if way:
            scan_state(way)

        def go(d, carry):
            to = (g + d) % GROUP
            copy_to(state.at[way, to], slices.at[way, g], s1_send.at[way, d], s1_recv.at[way, g],
                    (y * GROUP + to, x)).start()
            return carry

        lax.fori_loop(1, GROUP, go, 0)
        slices[way, g] = state[way, g]

    def scan_term(way, h):
        if way == 0:
            return dot(k_ref[:, head(h)], v_ref[:, head(h)], 0, 0)
        return dot(q_ref[:, head(h)], ga[:, head(h)], 0, 0)

    def scan_totals(way):
        def arrive(d, carry):
            at = (g + d) % GROUP
            copy_to(slices.at[way, at], slices.at[way, at], s1_send.at[way, d], s1_recv.at[way, at], sibling).wait_recv()
            return carry

        lax.fori_loop(1, GROUP, arrive, 0)
        run = jnp.zeros((SLICE, HDIM), F32)
        for i in (range(GROUP) if way == 0 else range(GROUP - 1, -1, -1)):
            partial[way, i] = run
            run = run + slices[way, i].astype(F32)
        totals[way, y] = run
        for d in range(1, NY):
            send(totals.at[way, y], totals.at[way, y], s2_send.at[way, d], s2_recv.at[way, y],
                 dev(x, (y + d) % NY, z, core))

    def scan_back(way):
        for d in range(1, NY):
            at = (y + d) % NY
            copy_to(totals.at[way, at], totals.at[way, at], s2_send.at[way, d], s2_recv.at[way, at], sibling).wait_recv()
        offset = jnp.zeros((SLICE, HDIM), F32)
        for j in range(NY):
            counts = (j < y) if way == 0 else (j > y)
            offset = offset + jnp.where(counts, totals[way, j], 0.0)
        for i in range(GROUP):
            back[way, i] = (partial[way, i] + offset).astype(BF16)

        def go(d, carry):
            to = (g + d) % GROUP
            copy_to(back.at[way, to], states.at[way, g], s3_send.at[way, d], s3_recv.at[way, g],
                    (y * GROUP + to, x)).start()
            return carry

        lax.fori_loop(1, GROUP, go, 0)
        states[way, g] = back[way, g]

    def scan_end(way):
        def arrive(d, carry):
            at = (g + d) % GROUP
            copy_to(states.at[way, at], states.at[way, at], s3_send.at[way, d], s3_recv.at[way, at], sibling).wait_recv()
            return carry

        lax.fori_loop(1, GROUP, arrive, 0)

    def state_of(way, h):
        n = HDIM // SLICE
        return states[way, h * n:(h + 1) * n].reshape(HDIM, HDIM)


    gain = g_ref[...].astype(F32)
    row = lax.broadcasted_iota(jnp.int32, (ROWS, ROWS), 0)
    col = lax.broadcasted_iota(jnp.int32, (ROWS, ROWS), 1)

    def local_attention(h):
        s = dot(q_ref[:, head(h)], k_ref[:, head(h)], 1, 1)
        m = jnp.where(row >= col, s, 0.0).astype(BF16)
        att[:, head(h)] = dot(m, v_ref[:, head(h)], 1, 0)

    def attend():
        for h in range(HEADS):
            a = att[:, head(h)] + dot(q_ref[:, head(h)], state_of(0, h), 1, 0)
            scale = lax.rsqrt(jnp.mean(a * a, axis=-1, keepdims=True) + EPS)
            a = a * scale
            att[:, head(h)] = a
            inv[h] = scale
            normed[x, :, head(h)] = (a * gain[:, head(h)]).astype(BF16)


    def cot_of(p):
        return c_ref[...] if p == 0 else ca[quarters[p]]

    def pair_go(p):
        cot_t[...] = cot_of(p).T.reshape(NZ, 2, PIECE, ROWS)
        other = cot_t[:, 1 - core].reshape(ROWS, ROWS)
        pair_stage[p] = dot(other, normed[x], 1, 0).astype(BF16).reshape(NZ, PIECE, ROWS)
        send(pair_stage.at[p], pair_recv.at[p], pair_send.at[p], pair_rsem.at[p], sibling)

    def pair_mine(p):
        mine = cot_t[:, core].reshape(ROWS, ROWS)
        dsum[p] = dot(mine, normed[x], 1, 0).reshape(NZ, PIECE, ROWS)

    def pair_end(p):
        copy_to(pair_stage.at[p], pair_recv.at[p], pair_send.at[p], pair_rsem.at[p], sibling).wait_recv()
        dsum[p] = dsum[p] + pair_recv[p].astype(F32)

    def ring_wait(p, i):
        copy_to(ring_stage.at[p, i], ring_recv.at[p, i], ring_send.at[p, i], ring_rsem.at[p, i], sibling).wait_recv()

    def ring_step(p, s):
        at = (z + step * (4 - s) + NZ) % NZ
        term = dsum[p, at]
        if s:
            ring_wait(p, s - 1)
            term = term + ring_recv[p, s - 1].astype(F32)
        ring_stage[p, s] = term.astype(BF16)
        send(ring_stage.at[p, s], ring_recv.at[p, s], ring_send.at[p, s], ring_rsem.at[p, s], d_major)
        if s < 3:
            at = (z - step * (3 - s) + NZ) % NZ
            term = dsum[p, at]
            if s:
                ring_wait(p, 3 + s)
                term = term + ring_recv[p, 3 + s].astype(F32)
            i = 4 + s
            ring_stage[p, i] = term.astype(BF16)
            send(ring_stage.at[p, i], ring_recv.at[p, i], ring_send.at[p, i], ring_rsem.at[p, i], d_minor)

    def ring_end(p):
        ring_wait(p, 3)
        ring_wait(p, 6)
        total = dsum[p, z] + ring_recv[p, 3].astype(F32) + ring_recv[p, 6].astype(F32)
        last_stage[p] = total.astype(BF16)
        a = quarters[p]

        @pl.when(a != y)
        def _():
            copy_to(last_stage.at[p], last_recv.at[y], last_send.at[p], last_rsem.at[y], dev(x, a, z, core)).start()

        @pl.when(a == y)
        def _():
            last_recv[y] = last_stage[p]

    quarters = (x, (x + 3) % NX, (x + 1) % NX, x_opp)

    def gn_part(p):
        w = wt[:, :, quarters[p]].reshape(NZ * 2 * PIECE, ROWS)
        part = dot(cot_of(p), w, 1, 0)
        gn[...] = part if p == 0 else gn[...] + part

    def gradient():
        for h in range(HEADS):
            w = gn[:, head(h)] * gain[:, head(h)]
            a = att[:, head(h)]
            along = jnp.mean(w * a, axis=-1, keepdims=True)
            ga[:, head(h)] = (inv[h] * (w - a * along)).astype(BF16)

    def queries_gradient(h):
        s = dot(ga[:, head(h)], v_ref[:, head(h)], 1, 1)
        m = jnp.where(row >= col, s, 0.0).astype(BF16)
        t = dot(m, k_ref[:, head(h)], 1, 0) + dot(ga[:, head(h)], state_of(0, h), 1, 1)
        gq_ref[:, head(h)] = t.astype(BF16)

    def local_keys_values(h):
        s = dot(v_ref[:, head(h)], ga[:, head(h)], 1, 1)
        m = jnp.where(col >= row, s, 0.0).astype(BF16)
        gn[:, head(h)] = dot(m, q_ref[:, head(h)], 1, 0)
        s = dot(k_ref[:, head(h)], q_ref[:, head(h)], 1, 1)
        m = jnp.where(col >= row, s, 0.0).astype(BF16)
        att[:, head(h)] = dot(m, ga[:, head(h)], 1, 0)

    def finish():
        for h in range(HEADS):
            st = state_of(1, h)
            gk_ref[:, head(h)] = (gn[:, head(h)] + dot(v_ref[:, head(h)], st, 1, 1)).astype(BF16)
            gv_ref[:, head(h)] = (att[:, head(h)] + dot(k_ref[:, head(h)], st, 1, 0)).astype(BF16)


    def layer_out():
        def out_rows(i, carry):
            r = pl.ds(pl.multiple_of(i * 128, 128), 128)
            total = jnp.zeros((128, NZ * 2 * PIECE), F32)
            for a in range(NX):
                total = total + dot(normed[a, r, :], wc[a].reshape(NZ * 2 * PIECE, ROWS), 1, 1)
            out_ref[r, :] = total.astype(BF16)
            return carry

        lax.fori_loop(0, ROWS // 128, out_rows, 0)


    def gw_sum():
        for d in range(1, NY):
            j = (y + d) % NY
            copy_to(last_stage.at[0], last_recv.at[j], last_send.at[0], last_rsem.at[j], sibling).wait_recv()
        gw_ref[...] = (
            (last_recv[0].astype(F32) + last_recv[1].astype(F32))
            + (last_recv[2].astype(F32) + last_recv[3].astype(F32))
        )

    scan_state(0)
    local_attention(0)
    local_attention(1)
    local_attention(2)
    wt[z, core, y] = w_ref[...]

    @pl.when(x == y)
    def _():
        wc[x, z, core] = w_ref[...]

    pl.semaphore_wait(barrier, (GROUP - 1) + (NY - 1) + 3 - me_diag.astype(jnp.int32))

    @pl.when(x != y)
    def _():
        copy_to(w_ref, wc.at[x, z, core], pm_send.at[0], pm_recv.at[0], dev(y, x, z, core)).start()

    ring_cot[0].start(c_ref.at[rows[0]])
    local_attention(3)
    ring_bz.start()
    ring_ay.start()
    scan_start(0)
    ring_cot[1].start(c_ref.at[rows[1]])
    ring_bz.go(1)
    ring_ay.go(1)
    turned()
    ring_cz.start()
    ring_ay.go(2)
    ring_az.start()
    ring_bz.go(2)
    scan_totals(0)
    ring_cz.go(1)
    ring_bz.go(3)
    scan_back(0)
    ring_az.go(1)
    ring_bz.go(4)
    ring_by.start()
    ring_cz.go(2)
    scan_end(0)
    attend()
    ring_cz.go(3)
    pair_go(0)
    pair_mine(0)
    ring_az.go(2)
    ring_by.go(1)
    ring_cz.go(4)
    pair_end(0)
    ring_step(0, 0)
    ring_cot[0].go(1)
    ring_cot[1].go(1)
    pair_go(1)
    pair_mine(1)
    ring_az.go(3)
    ring_by.go(2)
    ring_cy.start()
    ring_step(0, 1)
    pair_end(1)
    ring_step(1, 0)
    exchanged(NY, lambda i: by_view(i, 1 - core), bc_send, bc_recv)
    ring_az.go(4)
    ring_step(0, 2)
    exchanged(NZ, lambda i: az_view(i, 1 - core), ac_send, ac_recv)
    pair_go(2)
    ring_step(1, 1)
    pair_mine(2)
    gn_part(0)
    gn_part(1)
    ring_step(0, 3)
    pair_end(2)
    ring_cot[0].go(2)
    ring_n.start()
    ring_step(2, 0)
    gn_part(2)
    ring_cot[1].go(2)
    pair_go(3)
    pair_mine(3)
    ring_step(1, 2)
    gn_part(3)
    ring_end(0)
    gradient()
    pair_end(3)
    ring_step(3, 0)
    ring_cy.go(1)
    scan_start(1)
    ring_step(2, 1)
    local_keys_values(0)
    ring_step(1, 3)
    local_keys_values(1)
    local_keys_values(2)
    local_keys_values(3)
    queries_gradient(0)
    ring_step(3, 1)
    queries_gradient(1)
    queries_gradient(2)
    queries_gradient(3)
    ring_step(2, 2)
    ring_end(1)
    scan_totals(1)
    ring_cy.go(2)
    ring_step(3, 2)
    ring_n.go(1)
    ring_step(2, 3)
    exchanged(NY, lambda i: cy_view(i, 1 - core), cc_send, cc_recv)
    scan_back(1)
    ring_step(3, 3)
    ring_end(2)
    ring_end(3)
    ring_n.go(2)
    layer_out()
    scan_end(1)
    finish()
    gw_sum()

    for c in sent:
        c.wait_send()

    @pl.when(x != y)
    def _():
        copy_to(w_ref, wc.at[x, z, core], pm_send.at[0], pm_recv.at[0], sibling).wait_send()

    for p in range(NX):
        @pl.when(quarters[p] != y)
        def _():
            copy_to(last_stage.at[p], last_recv.at[y], last_send.at[p], last_rsem.at[y], sibling).wait_send()

    def left(d, carry):
        for way in range(2):
            to = (g + d) % GROUP
            copy_to(state.at[way, to], slices.at[way, g], s1_send.at[way, d], s1_recv.at[way, g], sibling).wait_send()
            copy_to(back.at[way, to], states.at[way, g], s3_send.at[way, d], s3_recv.at[way, g], sibling).wait_send()
        return carry

    lax.fori_loop(1, GROUP, left, 0)


def settle(*refs):
    n = (len(refs) - 1) // 3
    sems = refs[-1]
    come = [pltpu.make_async_copy(refs[i], refs[2 * n + i], sems.at[0, i]) for i in range(n)]
    go = [pltpu.make_async_copy(refs[2 * n + i], refs[n + i], sems.at[1, i]) for i in range(n)]
    for c in come:
        c.start()
    for i in range(n):
        come[i].wait()
        go[i].start()
    for c in go:
        c.wait()


def on_device(queries, keys, values, gain, out_weight, cotangent):
    width = HEADS * HDIM
    cols = NZ * 2 * PIECE
    vmem = pl.BlockSpec(memory_space=pltpu.VMEM)
    dma = pltpu.SemaphoreType.DMA
    outs = pl.pallas_call(
        kernel,
        out_shape=(
            jax.ShapeDtypeStruct((ROWS, cols), BF16),
            jax.ShapeDtypeStruct((ROWS, width), BF16),
            jax.ShapeDtypeStruct((ROWS, width), BF16),
            jax.ShapeDtypeStruct((ROWS, width), BF16),
            jax.ShapeDtypeStruct((PIECE, width), F32),
        ),
        in_specs=[vmem] * 6,
        out_specs=(vmem,) * 5,
        scratch_shapes=[
            pltpu.VMEM((NZ, 2, NY, PIECE, width), BF16),
            pltpu.VMEM((NX, NZ, 2, PIECE, width), BF16),
            pltpu.VMEM((NX, ROWS, cols), BF16),
            pltpu.VMEM((2, GROUP, SLICE, HDIM), BF16),
            pltpu.VMEM((2, GROUP, SLICE, HDIM), BF16),
            pltpu.VMEM((2, GROUP, SLICE, HDIM), F32),
            pltpu.VMEM((2, NY, SLICE, HDIM), F32),
            pltpu.VMEM((2, GROUP, SLICE, HDIM), BF16),
            pltpu.VMEM((2, GROUP, SLICE, HDIM), BF16),
            pltpu.VMEM((ROWS, width), F32),
            pltpu.VMEM((HEADS, ROWS, 1), F32),
            pltpu.VMEM((NX, ROWS, width), BF16),
            pltpu.VMEM((NZ, 2, PIECE, ROWS), BF16),
            pltpu.VMEM((ROWS, width), F32),
            pltpu.VMEM((ROWS, width), BF16),
            pltpu.VMEM((NX, NZ, PIECE, width), BF16),
            pltpu.VMEM((NX, NZ, PIECE, width), BF16),
            pltpu.VMEM((NX, NZ, PIECE, width), F32),
            pltpu.VMEM((NX, 7, PIECE, width), BF16),
            pltpu.VMEM((NX, 7, PIECE, width), BF16),
            pltpu.VMEM((NX, PIECE, width), BF16),
            pltpu.VMEM((NY, PIECE, width), BF16),
            dma((3,)), dma((3,)), dma((7,)), dma((7,)), dma((NZ,)), dma((NZ,)),
            dma((7,)), dma((7,)), dma((3,)), dma((3,)), dma((NY,)), dma((NY,)),
            dma((1,)), dma((1,)), dma((7,)), dma((7,)), dma((3,)), dma((3,)), dma((NY,)), dma((NY,)),
            dma((2, 3)), dma((2, 3)),
            dma((2, GROUP)), dma((2, GROUP)), dma((2, NY)), dma((2, NY)), dma((2, GROUP)), dma((2, GROUP)),
            dma((3,)), dma((3,)), dma((NX,)), dma((NX,)),
            dma((NX, 7)), dma((NX, 7)), dma((NX,)), dma((NY,)),
        ],
        compiler_params=pltpu.CompilerParams(
            collective_id=0, has_side_effects=True, vmem_limit_bytes=56 * 1024 * 1024
        ),
    )(queries, keys, values, gain.reshape(1, width), out_weight.T, cotangent)
    anywhere = pl.BlockSpec(memory_space=pl.ANY)
    outs = pl.pallas_call(
        settle,
        out_shape=tuple(jax.ShapeDtypeStruct(o.shape, o.dtype) for o in outs),
        in_specs=[anywhere] * len(outs),
        out_specs=(anywhere,) * len(outs),
        scratch_shapes=[pltpu.VMEM(o.shape, o.dtype) for o in outs] + [dma((2, len(outs)))],
    )(*outs)
    return outs[:4] + (outs[4].T,)


def solution(mesh):
    in_specs = (
        P("ctx", "head"),
        P("ctx", "head"),
        P("ctx", "head"),
        P("head"),
        P("head", "ctx"),
        P("ctx", "head"),
    )
    out_specs = (
        P("ctx", "head"),
        P("ctx", "head"),
        P("ctx", "head"),
        P("ctx", "head"),
        P("head", "ctx"),
    )
    return jax.shard_map(
        on_device, mesh=mesh, in_specs=in_specs, out_specs=out_specs, check_vma=False
    )
```

```python
import jax
import jax.numpy as jnp
from jax import lax
from jax.experimental import pallas as pl
from jax.experimental.pallas import tpu as pltpu
from jax.sharding import PartitionSpec as P

HDIM = 128
HEADS = 4
ROWS = 512
NX, NY, NZ = 4, 4, 8
GROUP = 2 * NZ
SLICE = HEADS * HDIM // GROUP
PIECE = 64
EPS = 1e-06
MESH = pl.DeviceIdType.MESH
F32, BF16 = jnp.float32, jnp.bfloat16


def dot(a, b, ca, cb):
    return lax.dot_general(a, b, (((ca,), (cb,)), ((), ())), preferred_element_type=F32)


def copy_to(src, dst, send_sem, recv_sem, device):
    return pltpu.make_async_remote_copy(
        src_ref=src, dst_ref=dst, send_sem=send_sem, recv_sem=recv_sem,
        device_id=device, device_id_type=MESH,
    )


def head(h):
    return slice(h * HDIM, (h + 1) * HDIM)


class Ring:
    def __init__(self, n, at, step, view, send_sem, recv_sem, device, sent, landed=None):
        self.n, self.at, self.step, self.view = n, at, step, view
        self.sems = send_sem, recv_sem
        self.major, self.minor = device((at + step + n) % n), device((at - step + n) % n)
        self.sent, self.landed = sent, landed

    def send(self, i, src, place, way):
        c = copy_to(src, self.view(place), self.sems[0].at[i], self.sems[1].at[i], way)
        c.start()
        self.sent.append(c)

    def arrive(self, i, place):
        view = self.view(place)
        copy_to(view, view, self.sems[0].at[i], self.sems[1].at[i], self.major).wait_recv()

    def start(self, src=None):
        src = self.view(self.at) if src is None else src
        self.send(0, src, self.at, self.major)
        self.send(self.n // 2, src, self.at, self.minor)
        if self.landed:
            self.landed(self.at)

    def go(self, s):
        n, half = self.n, self.n // 2
        places = [((self.at - self.step * s + n) % n, s - 1, s, self.major, s < half)]
        if s < half:
            places.append(((self.at + self.step * s + n) % n, half + s - 1, half + s, self.minor, s < half - 1))
        for place, came, goes, way, more in places:
            self.arrive(came, place)
            if more:
                self.send(goes, self.view(place), place, way)
            if self.landed:
                self.landed(place)


def kernel(
    q_in, k_in, v_in, g_ref, w_ref, c_in,
    out_ref, gq_ref, gk_ref, gv_ref, gw_ref,
    q_ref, k_ref, v_ref, c_ref, wt, wc, ca, state, slices, partial, totals, back, states,
    att, inv, normed, cot_t, gn, ga, acc,
    pair_stage, pair_recv, dsum, ring_stage, ring_recv, last_stage, last_recv,
    in_sem, ay_send, ay_recv, az_send, az_recv, ac_send, ac_recv,
    bz_send, bz_recv, by_send, by_recv, bc_send, bc_recv,
    pm_send, pm_recv, cz_send, cz_recv, cy_send, cy_recv, cc_send, cc_recv,
    ca_send, ca_recv,
    s1_send, s1_recv, s2_send, s2_recv, s3_send, s3_recv,
    n_send, n_recv, pair_send, pair_rsem,
    ring_send, ring_rsem, last_send, last_rsem,
):
    ctx, x = lax.axis_index("ctx"), lax.axis_index("head")
    y, z, core = ctx // GROUP, (ctx // 2) % NZ, ctx % 2
    g = ctx % GROUP
    me_diag = x == y

    def dev(x, y, z, core):
        return (y * GROUP + z * 2 + core, x)

    step = 1 - 2 * core
    z_major, z_minor = (z + step + NZ) % NZ, (z - step + NZ) % NZ
    x_opp = (x + 2) % NX
    d_major, d_minor = dev(x, y, z_major, core), dev(x, y, z_minor, core)
    sibling = dev(x, y, z, 1 - core)
    sent = []

    def send(*args):
        c = copy_to(*args)
        c.start()
        sent.append(c)

    barrier = pltpu.get_barrier_semaphore()

    def hello(device):
        pl.semaphore_signal(barrier, inc=1, device_id=device, device_id_type=MESH)

    def hello_group(d, carry):
        hello((y * GROUP + (g + d) % GROUP, x))
        return carry

    lax.fori_loop(1, GROUP, hello_group, 0)
    for d in range(1, NY):
        hello(dev(x, (y + d) % NY, z, core))
    hello(dev((x + 1) % NX, y, z, core))
    hello(dev((x + 3) % NX, y, z, core))

    @pl.when(x != y)
    def _():
        hello(dev(y, x, z, core))


    inputs = [
        pltpu.make_async_copy(there, here, in_sem.at[i])
        for i, (there, here) in enumerate(
            ((k_in, k_ref), (v_in, v_ref), (q_in, q_ref), (w_ref, wt.at[z, core, y]), (c_in, c_ref))
        )
    ]
    for c in inputs:
        c.start()

    def on_y(j):
        return dev(x, j, z, core)

    def on_z(j):
        return dev(x, y, j, core)

    def on_x(j):
        return dev(j, y, z, core)

    def exchange(view, send_sem, recv_sem):
        def landed(place):
            send(view(place), view(place), send_sem.at[place], recv_sem.at[place], sibling)

        return landed

    def exchanged(n, view, send_sem, recv_sem):
        for i in range(n):
            copy_to(view(i), view(i), send_sem.at[i], recv_sem.at[i], sibling).wait_recv()

    half = PIECE // 2
    low, high = pl.ds(0, half), pl.ds(half, half)
    az_view = lambda i, c=core: wt.at[i, c, :, low]
    by_view = lambda i, c=core: wt.at[:, c, i, high]
    cy_view = lambda i, c=core: wc.at[i, :, c]
    ring_ay = Ring(NY, y, step, lambda i: wt.at[z, core, i, low], ay_send, ay_recv, on_y, sent)
    ring_az = Ring(NZ, z, step, az_view, az_send, az_recv, on_z, sent, exchange(az_view, ac_send, ac_recv))
    ring_bz = Ring(NZ, z, step, lambda i: wt.at[i, core, y, high], bz_send, bz_recv, on_z, sent)
    ring_by = Ring(NY, y, step, by_view, by_send, by_recv, on_y, sent, exchange(by_view, bc_send, bc_recv))
    ring_cz = Ring(NZ, z, step, lambda i: wc.at[y, i, core], cz_send, cz_recv, on_z, sent)
    ring_cy = Ring(NY, y, step, cy_view, cy_send, cy_recv, on_y, sent, exchange(cy_view, cc_send, cc_recv))
    rows = [pl.ds(0, ROWS // 2), pl.ds(ROWS // 2, ROWS // 2)]
    ring_cot = [
        Ring(NX, x, step, lambda i, r=r: ca.at[i, r], ca_send.at[h], ca_recv.at[h], on_x, sent)
        for h, r in enumerate(rows)
    ]
    ring_n = Ring(NX, x, step, lambda i: normed.at[i], n_send, n_recv, on_x, sent)

    def turned():
        @pl.when(x != y)
        def _():
            copy_to(w_ref, wc.at[y, z, core], pm_send.at[0], pm_recv.at[0], sibling).wait_recv()

    def scan_state(way):
        for h in range(HEADS):
            state[way, h * (HDIM // SLICE):(h + 1) * (HDIM // SLICE)] = (
                scan_term(way, h).astype(BF16).reshape(HDIM // SLICE, SLICE, HDIM)
            )

    def scan_start(way):
        if way:
            scan_state(way)

        def go(d, carry):
            to = (g + d) % GROUP
            copy_to(state.at[way, to], slices.at[way, g], s1_send.at[way, d], s1_recv.at[way, g],
                    (y * GROUP + to, x)).start()
            return carry

        lax.fori_loop(1, GROUP, go, 0)
        slices[way, g] = state[way, g]

    def scan_term(way, h):
        if way == 0:
            return dot(k_ref[:, head(h)], v_ref[:, head(h)], 0, 0)
        return dot(q_ref[:, head(h)], ga[:, head(h)], 0, 0)

    def scan_totals(way):
        def arrive(d, carry):
            at = (g + d) % GROUP
            copy_to(slices.at[way, at], slices.at[way, at], s1_send.at[way, d], s1_recv.at[way, at], sibling).wait_recv()
            return carry

        lax.fori_loop(1, GROUP, arrive, 0)
        run = jnp.zeros((SLICE, HDIM), F32)
        for i in (range(GROUP) if way == 0 else range(GROUP - 1, -1, -1)):
            partial[way, i] = run
            run = run + slices[way, i].astype(F32)
        totals[way, y] = run
        for d in range(1, NY):
            send(totals.at[way, y], totals.at[way, y], s2_send.at[way, d], s2_recv.at[way, y],
                 dev(x, (y + d) % NY, z, core))

    def scan_back(way):
        for d in range(1, NY):
            at = (y + d) % NY
            copy_to(totals.at[way, at], totals.at[way, at], s2_send.at[way, d], s2_recv.at[way, at], sibling).wait_recv()
        offset = jnp.zeros((SLICE, HDIM), F32)
        for j in range(NY):
            counts = (j < y) if way == 0 else (j > y)
            offset = offset + jnp.where(counts, totals[way, j], 0.0)
        for i in range(GROUP):
            back[way, i] = (partial[way, i] + offset).astype(BF16)

        def go(d, carry):
            to = (g + d) % GROUP
            copy_to(back.at[way, to], states.at[way, g], s3_send.at[way, d], s3_recv.at[way, g],
                    (y * GROUP + to, x)).start()
            return carry

        lax.fori_loop(1, GROUP, go, 0)
        states[way, g] = back[way, g]

    def scan_end(way):
        def arrive(d, carry):
            at = (g + d) % GROUP
            copy_to(states.at[way, at], states.at[way, at], s3_send.at[way, d], s3_recv.at[way, at], sibling).wait_recv()
            return carry

        lax.fori_loop(1, GROUP, arrive, 0)

    def state_of(way, h):
        n = HDIM // SLICE
        return states[way, h * n:(h + 1) * n].reshape(HDIM, HDIM)


    gain = g_ref[...].astype(F32).reshape(1, HEADS * HDIM)
    row = lax.broadcasted_iota(jnp.int32, (ROWS, ROWS), 0)
    col = lax.broadcasted_iota(jnp.int32, (ROWS, ROWS), 1)

    def local_attention(h):
        s = dot(q_ref[:, head(h)], k_ref[:, head(h)], 1, 1)
        m = jnp.where(row >= col, s, 0.0).astype(BF16)
        att[:, head(h)] = dot(m, v_ref[:, head(h)], 1, 0)

    def attend():
        for h in range(HEADS):
            a = att[:, head(h)] + dot(q_ref[:, head(h)], state_of(0, h), 1, 0)
            scale = lax.rsqrt(jnp.mean(a * a, axis=-1, keepdims=True) + EPS)
            a = a * scale
            att[:, head(h)] = a
            inv[h] = scale
            normed[x, :, head(h)] = (a * gain[:, head(h)]).astype(BF16)


    def cot_of(p):
        return c_ref[...] if p == 0 else ca[quarters[p]]

    def pair_go(p):
        cot_t[...] = cot_of(p).T.reshape(NZ, 2, PIECE, ROWS)
        other = cot_t[:, 1 - core].reshape(ROWS, ROWS)
        pair_stage[p] = dot(other, normed[x], 1, 0).astype(BF16).reshape(NZ, PIECE, ROWS)
        send(pair_stage.at[p], pair_recv.at[p], pair_send.at[p], pair_rsem.at[p], sibling)

    def pair_mine(p):
        mine = cot_t[:, core].reshape(ROWS, ROWS)
        dsum[p] = dot(mine, normed[x], 1, 0).reshape(NZ, PIECE, ROWS)

    def pair_end(p):
        copy_to(pair_stage.at[p], pair_recv.at[p], pair_send.at[p], pair_rsem.at[p], sibling).wait_recv()
        dsum[p] = dsum[p] + pair_recv[p].astype(F32)

    def ring_wait(p, i):
        copy_to(ring_stage.at[p, i], ring_recv.at[p, i], ring_send.at[p, i], ring_rsem.at[p, i], sibling).wait_recv()

    def ring_step(p, s):
        at = (z + step * (4 - s) + NZ) % NZ
        term = dsum[p, at]
        if s:
            ring_wait(p, s - 1)
            term = term + ring_recv[p, s - 1].astype(F32)
        ring_stage[p, s] = term.astype(BF16)
        send(ring_stage.at[p, s], ring_recv.at[p, s], ring_send.at[p, s], ring_rsem.at[p, s], d_major)
        if s < 3:
            at = (z - step * (3 - s) + NZ) % NZ
            term = dsum[p, at]
            if s:
                ring_wait(p, 3 + s)
                term = term + ring_recv[p, 3 + s].astype(F32)
            i = 4 + s
            ring_stage[p, i] = term.astype(BF16)
            send(ring_stage.at[p, i], ring_recv.at[p, i], ring_send.at[p, i], ring_rsem.at[p, i], d_minor)

    def ring_end(p):
        ring_wait(p, 3)
        ring_wait(p, 6)
        total = dsum[p, z] + ring_recv[p, 3].astype(F32) + ring_recv[p, 6].astype(F32)
        last_stage[p] = total.astype(BF16)
        a = quarters[p]

        @pl.when(a != y)
        def _():
            copy_to(last_stage.at[p], last_recv.at[y], last_send.at[p], last_rsem.at[y], dev(x, a, z, core)).start()

        @pl.when(a == y)
        def _():
            last_recv[y] = last_stage[p]

    quarters = (x, (x + 3) % NX, (x + 1) % NX, x_opp)

    def gn_part(p):
        w = wt[:, :, quarters[p]].reshape(NZ * 2 * PIECE, ROWS)
        part = dot(cot_of(p), w, 1, 0)
        gn[...] = part if p == 0 else gn[...] + part

    def gradient():
        for h in range(HEADS):
            w = gn[:, head(h)] * gain[:, head(h)]
            a = att[:, head(h)]
            along = jnp.mean(w * a, axis=-1, keepdims=True)
            ga[:, head(h)] = (inv[h] * (w - a * along)).astype(BF16)

    def queries_gradient(h):
        s = dot(ga[:, head(h)], v_ref[:, head(h)], 1, 1)
        m = jnp.where(row >= col, s, 0.0).astype(BF16)
        t = dot(m, k_ref[:, head(h)], 1, 0) + dot(ga[:, head(h)], state_of(0, h), 1, 1)
        gq_ref[:, head(h)] = t.astype(BF16)

    def local_keys_values(h):
        s = dot(v_ref[:, head(h)], ga[:, head(h)], 1, 1)
        m = jnp.where(col >= row, s, 0.0).astype(BF16)
        gn[:, head(h)] = dot(m, q_ref[:, head(h)], 1, 0)
        s = dot(k_ref[:, head(h)], q_ref[:, head(h)], 1, 1)
        m = jnp.where(col >= row, s, 0.0).astype(BF16)
        att[:, head(h)] = dot(m, ga[:, head(h)], 1, 0)

    def finish():
        for h in range(HEADS):
            st = state_of(1, h)
            gk_ref[:, head(h)] = (gn[:, head(h)] + dot(v_ref[:, head(h)], st, 1, 1)).astype(BF16)
            gv_ref[:, head(h)] = (att[:, head(h)] + dot(k_ref[:, head(h)], st, 1, 0)).astype(BF16)


    def out_part(p):
        a = quarters[p]
        part = dot(normed[a], wc[a].reshape(NZ * 2 * PIECE, ROWS), 1, 1)
        if p:
            part = part + acc[...]
        if p < NX - 1:
            acc[...] = part
        else:
            out_ref[...] = part.astype(BF16)

    def gw_sum():
        for d in range(1, NY):
            j = (y + d) % NY
            copy_to(last_stage.at[0], last_recv.at[j], last_send.at[0], last_rsem.at[j], sibling).wait_recv()
        gw_ref[...] = (
            (last_recv[0].astype(F32) + last_recv[1].astype(F32))
            + (last_recv[2].astype(F32) + last_recv[3].astype(F32))
        )

    for c in inputs[:2]:
        c.wait()
    scan_state(0)
    inputs[2].wait()
    local_attention(0)
    local_attention(1)
    local_attention(2)
    inputs[3].wait()

    @pl.when(x == y)
    def _():
        turn = pltpu.make_async_copy(w_ref, wc.at[x, z, core], in_sem.at[5])
        turn.start()
        turn.wait()

    pl.semaphore_wait(barrier, (GROUP - 1) + (NY - 1) + 3 - me_diag.astype(jnp.int32))

    @pl.when(x != y)
    def _():
        copy_to(w_ref, wc.at[x, z, core], pm_send.at[0], pm_recv.at[0], dev(y, x, z, core)).start()

    ring_cot[0].start(c_in.at[rows[0]])
    ring_bz.start()
    scan_start(0)
    ring_cot[1].start(c_in.at[rows[1]])
    ring_ay.start()
    local_attention(3)
    ring_bz.go(1)
    ring_ay.go(1)
    turned()
    ring_cz.start()
    ring_bz.go(2)
    ring_ay.go(2)
    ring_az.start()
    scan_totals(0)
    ring_cz.go(1)
    ring_bz.go(3)
    scan_back(0)
    ring_az.go(1)
    ring_cot[0].go(1)
    ring_cz.go(2)
    ring_bz.go(4)
    ring_by.start()
    scan_end(0)
    attend()
    inputs[4].wait()
    pair_go(0)
    pair_mine(0)
    ring_cz.go(3)
    ring_az.go(2)
    pair_end(0)
    ring_step(0, 0)
    ring_by.go(1)
    ring_cz.go(4)
    ring_cot[1].go(1)
    pair_go(2)
    ring_az.go(3)
    pair_mine(2)
    ring_by.go(2)
    ring_cy.start()
    pair_go(1)
    ring_step(0, 1)
    pair_mine(1)
    pair_end(2)
    exchanged(NY, lambda i: by_view(i, 1 - core), bc_send, bc_recv)
    ring_step(2, 0)
    ring_az.go(4)
    pair_end(1)
    ring_step(1, 0)
    ring_cot[0].go(2)
    ring_n.start()
    exchanged(NZ, lambda i: az_view(i, 1 - core), ac_send, ac_recv)
    gn_part(0)
    gn_part(1)
    ring_step(0, 2)
    gn_part(2)
    ring_step(2, 1)
    ring_step(1, 1)
    ring_step(0, 3)
    ring_cot[1].go(2)
    pair_go(3)
    pair_mine(3)
    ring_step(2, 2)
    gn_part(3)
    gradient()
    pair_end(3)
    ring_step(3, 0)
    ring_end(0)
    scan_start(1)
    queries_gradient(0)
    ring_cy.go(1)
    queries_gradient(1)
    queries_gradient(2)
    queries_gradient(3)
    ring_step(1, 2)
    local_keys_values(0)
    local_keys_values(1)
    ring_step(3, 1)
    local_keys_values(2)
    local_keys_values(3)
    ring_step(2, 3)
    ring_step(1, 3)
    scan_totals(1)
    ring_step(3, 2)
    ring_end(2)
    ring_n.go(1)
    ring_end(1)
    ring_cy.go(2)
    ring_step(3, 3)
    scan_back(1)
    exchanged(NY, lambda i: cy_view(i, 1 - core), cc_send, cc_recv)
    out_part(0)
    out_part(1)
    out_part(2)
    ring_end(3)
    ring_n.go(2)
    out_part(3)
    scan_end(1)
    finish()
    gw_sum()

    for c in sent:
        c.wait_send()

    @pl.when(x != y)
    def _():
        copy_to(w_ref, wc.at[x, z, core], pm_send.at[0], pm_recv.at[0], sibling).wait_send()

    for p in range(NX):
        @pl.when(quarters[p] != y)
        def _():
            copy_to(last_stage.at[p], last_recv.at[y], last_send.at[p], last_rsem.at[y], sibling).wait_send()

    def left(d, carry):
        for way in range(2):
            to = (g + d) % GROUP
            copy_to(state.at[way, to], slices.at[way, g], s1_send.at[way, d], s1_recv.at[way, g], sibling).wait_send()
            copy_to(back.at[way, to], states.at[way, g], s3_send.at[way, d], s3_recv.at[way, g], sibling).wait_send()
        return carry

    lax.fori_loop(1, GROUP, left, 0)


def settle(*refs):
    n = (len(refs) - 1) // 2
    copies = [pltpu.make_async_copy(refs[i], refs[n + i], refs[-1].at[i]) for i in range(n)]
    for c in copies:
        c.start()
    for c in copies:
        c.wait()


def on_device(queries, keys, values, gain, out_weight, cotangent):
    width = HEADS * HDIM
    cols = NZ * 2 * PIECE
    vmem = pl.BlockSpec(memory_space=pltpu.VMEM)
    anywhere = pl.BlockSpec(memory_space=pl.ANY)
    hbm = pl.BlockSpec(memory_space=pltpu.HBM)
    dma = pltpu.SemaphoreType.DMA
    outs = pl.pallas_call(
        kernel,
        out_shape=(
            pltpu.VMEM((ROWS, cols), BF16),
            pltpu.VMEM((ROWS, width), BF16),
            pltpu.VMEM((ROWS, width), BF16),
            pltpu.VMEM((ROWS, width), BF16),
            pltpu.VMEM((PIECE, width), F32),
        ),
        in_specs=[hbm, hbm, hbm, vmem, hbm, hbm],
        out_specs=(vmem,) * 5,
        scratch_shapes=[
            pltpu.VMEM((ROWS, width), BF16),
            pltpu.VMEM((ROWS, width), BF16),
            pltpu.VMEM((ROWS, width), BF16),
            pltpu.VMEM((ROWS, cols), BF16),
            pltpu.VMEM((NZ, 2, NY, PIECE, width), BF16),
            pltpu.VMEM((NX, NZ, 2, PIECE, width), BF16),
            pltpu.VMEM((NX, ROWS, cols), BF16),
            pltpu.VMEM((2, GROUP, SLICE, HDIM), BF16),
            pltpu.VMEM((2, GROUP, SLICE, HDIM), BF16),
            pltpu.VMEM((2, GROUP, SLICE, HDIM), F32),
            pltpu.VMEM((2, NY, SLICE, HDIM), F32),
            pltpu.VMEM((2, GROUP, SLICE, HDIM), BF16),
            pltpu.VMEM((2, GROUP, SLICE, HDIM), BF16),
            pltpu.VMEM((ROWS, width), F32),
            pltpu.VMEM((HEADS, ROWS, 1), F32),
            pltpu.VMEM((NX, ROWS, width), BF16),
            pltpu.VMEM((NZ, 2, PIECE, ROWS), BF16),
            pltpu.VMEM((ROWS, width), F32),
            pltpu.VMEM((ROWS, width), BF16),
            pltpu.VMEM((ROWS, cols), F32),
            pltpu.VMEM((NX, NZ, PIECE, width), BF16),
            pltpu.VMEM((NX, NZ, PIECE, width), BF16),
            pltpu.VMEM((NX, NZ, PIECE, width), F32),
            pltpu.VMEM((NX, 7, PIECE, width), BF16),
            pltpu.VMEM((NX, 7, PIECE, width), BF16),
            pltpu.VMEM((NX, PIECE, width), BF16),
            pltpu.VMEM((NY, PIECE, width), BF16),
            dma((6,)),
            dma((3,)), dma((3,)), dma((7,)), dma((7,)), dma((NZ,)), dma((NZ,)),
            dma((7,)), dma((7,)), dma((3,)), dma((3,)), dma((NY,)), dma((NY,)),
            dma((1,)), dma((1,)), dma((7,)), dma((7,)), dma((3,)), dma((3,)), dma((NY,)), dma((NY,)),
            dma((2, 3)), dma((2, 3)),
            dma((2, GROUP)), dma((2, GROUP)), dma((2, NY)), dma((2, NY)), dma((2, GROUP)), dma((2, GROUP)),
            dma((3,)), dma((3,)), dma((NX,)), dma((NX,)),
            dma((NX, 7)), dma((NX, 7)), dma((NX,)), dma((NY,)),
        ],
        compiler_params=pltpu.CompilerParams(
            collective_id=0, has_side_effects=True, vmem_limit_bytes=60 * 1024 * 1024
        ),
    )(queries, keys, values, gain, out_weight.T, cotangent)
    outs = [pltpu.with_memory_space_constraint(o, pltpu.VMEM) for o in outs]
    outs = pl.pallas_call(
        settle,
        out_shape=tuple(jax.ShapeDtypeStruct(o.shape, o.dtype) for o in outs),
        in_specs=[vmem] * len(outs),
        out_specs=(anywhere,) * len(outs),
        scratch_shapes=[dma((len(outs),))],
        compiler_params=pltpu.CompilerParams(vmem_limit_bytes=1024 * 1024),
    )(*outs)
    return outs[:4] + (outs[4].T,)


def solution(mesh):
    in_specs = (
        P("ctx", "head"),
        P("ctx", "head"),
        P("ctx", "head"),
        P("head"),
        P("head", "ctx"),
        P("ctx", "head"),
    )
    out_specs = (
        P("ctx", "head"),
        P("ctx", "head"),
        P("ctx", "head"),
        P("ctx", "head"),
        P("head", "ctx"),
    )
    return jax.shard_map(
        on_device, mesh=mesh, in_specs=in_specs, out_specs=out_specs, check_vma=False
    )
```

```python
import jax
import jax.numpy as jnp
from jax import lax
from jax.experimental import pallas as pl
from jax.experimental.pallas import tpu as pltpu
from jax.sharding import PartitionSpec as P

HDIM = 128
HEADS = 4
ROWS = 512
NX, NY, NZ = 4, 4, 8
GROUP = 2 * NZ
SLICE = HEADS * HDIM // GROUP
PIECE = 64
EPS = 1e-06
MESH = pl.DeviceIdType.MESH
F32, BF16 = jnp.float32, jnp.bfloat16


def dot(a, b, ca, cb):
    return lax.dot_general(a, b, (((ca,), (cb,)), ((), ())), preferred_element_type=F32)


def copy_to(src, dst, send_sem, recv_sem, device):
    return pltpu.make_async_remote_copy(
        src_ref=src, dst_ref=dst, send_sem=send_sem, recv_sem=recv_sem,
        device_id=device, device_id_type=MESH,
    )


def head(h):
    return slice(h * HDIM, (h + 1) * HDIM)


class Ring:
    def __init__(self, n, at, step, view, send_sem, recv_sem, device, sent, landed=None):
        self.n, self.at, self.step, self.view = n, at, step, view
        self.sems = send_sem, recv_sem
        self.major, self.minor = device((at + step + n) % n), device((at - step + n) % n)
        self.sent, self.landed = sent, landed

    def send(self, i, src, place, way):
        c = copy_to(src, self.view(place), self.sems[0].at[i], self.sems[1].at[i], way)
        c.start()
        self.sent.append(c)

    def arrive(self, i, place):
        view = self.view(place)
        copy_to(view, view, self.sems[0].at[i], self.sems[1].at[i], self.major).wait_recv()

    def start(self, src=None):
        src = self.view(self.at) if src is None else src
        self.send(0, src, self.at, self.major)
        self.send(self.n // 2, src, self.at, self.minor)
        if self.landed:
            self.landed(self.at)

    def go(self, s):
        n, half = self.n, self.n // 2
        places = [((self.at - self.step * s + n) % n, s - 1, s, self.major, s < half)]
        if s < half:
            places.append(((self.at + self.step * s + n) % n, half + s - 1, half + s, self.minor, s < half - 1))
        for place, came, goes, way, more in places:
            self.arrive(came, place)
            if more:
                self.send(goes, self.view(place), place, way)
            if self.landed:
                self.landed(place)


def kernel(
    q_in, k_in, v_in, g_ref, w_ref, c_in,
    out_ref, gq_ref, gk_ref, gv_ref, gw_ref,
    q_ref, k_ref, v_ref, c_ref, wt, wc, ca, state, slices, partial, totals, back, states,
    att, inv, normed, cot_t, gn, ga, acc,
    pair_stage, pair_recv, dsum, ring_stage, ring_recv, last_stage, last_recv,
    in_sem, ay_send, ay_recv, az_send, az_recv, ac_send, ac_recv,
    bz_send, bz_recv, by_send, by_recv, bc_send, bc_recv,
    pm_send, pm_recv, cz_send, cz_recv, cy_send, cy_recv, cc_send, cc_recv,
    ca_send, ca_recv,
    s1_send, s1_recv, s2_send, s2_recv, s3_send, s3_recv,
    n_send, n_recv, pair_send, pair_rsem,
    ring_send, ring_rsem, last_send, last_rsem,
):
    ctx, x = lax.axis_index("ctx"), lax.axis_index("head")
    y, z, core = ctx // GROUP, (ctx // 2) % NZ, ctx % 2
    g = ctx % GROUP
    me_diag = x == y

    def dev(x, y, z, core):
        return (y * GROUP + z * 2 + core, x)

    step = 1 - 2 * core
    z_major, z_minor = (z + step + NZ) % NZ, (z - step + NZ) % NZ
    x_opp = (x + 2) % NX
    d_major, d_minor = dev(x, y, z_major, core), dev(x, y, z_minor, core)
    sibling = dev(x, y, z, 1 - core)
    sent = []

    def send(*args):
        c = copy_to(*args)
        c.start()
        sent.append(c)

    barrier = pltpu.get_barrier_semaphore()

    def hello(device):
        pl.semaphore_signal(barrier, inc=1, device_id=device, device_id_type=MESH)

    def hello_group(d, carry):
        hello((y * GROUP + (g + d) % GROUP, x))
        return carry

    lax.fori_loop(1, GROUP, hello_group, 0)
    for d in range(1, NY):
        hello(dev(x, (y + d) % NY, z, core))
    hello(dev((x + 1) % NX, y, z, core))
    hello(dev((x + 3) % NX, y, z, core))

    @pl.when(x != y)
    def _():
        hello(dev(y, x, z, core))


    inputs = [
        pltpu.make_async_copy(there, here, in_sem.at[i])
        for i, (there, here) in enumerate(
            ((k_in, k_ref), (v_in, v_ref), (q_in, q_ref), (w_ref, wt.at[z, core, y]), (c_in, c_ref))
        )
    ]
    for c in inputs:
        c.start()

    def on_y(j):
        return dev(x, j, z, core)

    def on_z(j):
        return dev(x, y, j, core)

    def on_x(j):
        return dev(j, y, z, core)

    def exchange(view, send_sem, recv_sem):
        def landed(place):
            send(view(place), view(place), send_sem.at[place], recv_sem.at[place], sibling)

        return landed

    def exchanged(n, view, send_sem, recv_sem):
        for i in range(n):
            copy_to(view(i), view(i), send_sem.at[i], recv_sem.at[i], sibling).wait_recv()

    half = PIECE // 2
    low, high = pl.ds(0, half), pl.ds(half, half)
    az_view = lambda i, c=core: wt.at[i, c, :, low]
    by_view = lambda i, c=core: wt.at[:, c, i, high]
    cy_view = lambda i, c=core: wc.at[i, :, c]
    ring_ay = Ring(NY, y, step, lambda i: wt.at[z, core, i, low], ay_send, ay_recv, on_y, sent)
    ring_az = Ring(NZ, z, step, az_view, az_send, az_recv, on_z, sent, exchange(az_view, ac_send, ac_recv))
    ring_bz = Ring(NZ, z, step, lambda i: wt.at[i, core, y, high], bz_send, bz_recv, on_z, sent)
    ring_by = Ring(NY, y, step, by_view, by_send, by_recv, on_y, sent, exchange(by_view, bc_send, bc_recv))
    ring_cz = Ring(NZ, z, step, lambda i: wc.at[y, i, core], cz_send, cz_recv, on_z, sent)
    ring_cy = Ring(NY, y, step, cy_view, cy_send, cy_recv, on_y, sent, exchange(cy_view, cc_send, cc_recv))
    rows = [pl.ds(0, ROWS // 2), pl.ds(ROWS // 2, ROWS // 2)]
    ring_cot = [
        Ring(NX, x, step, lambda i, r=r: ca.at[i, r], ca_send.at[h], ca_recv.at[h], on_x, sent)
        for h, r in enumerate(rows)
    ]
    ring_n = Ring(NX, x, step, lambda i: normed.at[i], n_send, n_recv, on_x, sent)

    def turned():
        @pl.when(x != y)
        def _():
            copy_to(w_ref, wc.at[y, z, core], pm_send.at[0], pm_recv.at[0], sibling).wait_recv()

    def scan_state(way):
        for h in range(HEADS):
            state[way, h * (HDIM // SLICE):(h + 1) * (HDIM // SLICE)] = (
                scan_term(way, h).astype(BF16).reshape(HDIM // SLICE, SLICE, HDIM)
            )

    def scan_start(way):
        if way:
            scan_state(way)

        def go(d, carry):
            to = (g + d) % GROUP
            copy_to(state.at[way, to], slices.at[way, g], s1_send.at[way, d], s1_recv.at[way, g],
                    (y * GROUP + to, x)).start()
            return carry

        lax.fori_loop(1, GROUP, go, 0)
        slices[way, g] = state[way, g]

    def scan_term(way, h):
        if way == 0:
            return dot(k_ref[:, head(h)], v_ref[:, head(h)], 0, 0)
        return dot(q_ref[:, head(h)], ga[:, head(h)], 0, 0)

    def scan_totals(way):
        def arrive(d, carry):
            at = (g + d) % GROUP
            copy_to(slices.at[way, at], slices.at[way, at], s1_send.at[way, d], s1_recv.at[way, at], sibling).wait_recv()
            return carry

        lax.fori_loop(1, GROUP, arrive, 0)
        run = jnp.zeros((SLICE, HDIM), F32)
        for i in (range(GROUP) if way == 0 else range(GROUP - 1, -1, -1)):
            partial[way, i] = run
            run = run + slices[way, i].astype(F32)
        totals[way, y] = run
        for d in range(1, NY):
            send(totals.at[way, y], totals.at[way, y], s2_send.at[way, d], s2_recv.at[way, y],
                 dev(x, (y + d) % NY, z, core))

    def scan_back(way):
        for d in range(1, NY):
            at = (y + d) % NY
            copy_to(totals.at[way, at], totals.at[way, at], s2_send.at[way, d], s2_recv.at[way, at], sibling).wait_recv()
        offset = jnp.zeros((SLICE, HDIM), F32)
        for j in range(NY):
            counts = (j < y) if way == 0 else (j > y)
            offset = offset + jnp.where(counts, totals[way, j], 0.0)
        for i in range(GROUP):
            back[way, i] = (partial[way, i] + offset).astype(BF16)

        def go(d, carry):
            to = (g + d) % GROUP
            copy_to(back.at[way, to], states.at[way, g], s3_send.at[way, d], s3_recv.at[way, g],
                    (y * GROUP + to, x)).start()
            return carry

        lax.fori_loop(1, GROUP, go, 0)
        states[way, g] = back[way, g]

    def scan_end(way):
        def arrive(d, carry):
            at = (g + d) % GROUP
            copy_to(states.at[way, at], states.at[way, at], s3_send.at[way, d], s3_recv.at[way, at], sibling).wait_recv()
            return carry

        lax.fori_loop(1, GROUP, arrive, 0)

    def state_of(way, h):
        n = HDIM // SLICE
        return states[way, h * n:(h + 1) * n].reshape(HDIM, HDIM)


    gain = g_ref[...].astype(F32).reshape(1, HEADS * HDIM)
    row = lax.broadcasted_iota(jnp.int32, (ROWS, ROWS), 0)
    col = lax.broadcasted_iota(jnp.int32, (ROWS, ROWS), 1)

    def local_attention(h):
        s = dot(q_ref[:, head(h)], k_ref[:, head(h)], 1, 1)
        m = jnp.where(row >= col, s, 0.0).astype(BF16)
        att[:, head(h)] = dot(m, v_ref[:, head(h)], 1, 0)

    def attend():
        for h in range(HEADS):
            a = att[:, head(h)] + dot(q_ref[:, head(h)], state_of(0, h), 1, 0)
            scale = lax.rsqrt(jnp.mean(a * a, axis=-1, keepdims=True) + EPS)
            a = a * scale
            att[:, head(h)] = a
            inv[h] = scale
            normed[x, :, head(h)] = (a * gain[:, head(h)]).astype(BF16)


    def cot_of(p):
        return c_ref[...] if p == 0 else ca[quarters[p]]

    def pair_go(p):
        cot_t[...] = cot_of(p).T.reshape(NZ, 2, PIECE, ROWS)
        other = cot_t[:, 1 - core].reshape(ROWS, ROWS)
        pair_stage[p] = dot(other, normed[x], 1, 0).astype(BF16).reshape(NZ, PIECE, ROWS)
        send(pair_stage.at[p], pair_recv.at[p], pair_send.at[p], pair_rsem.at[p], sibling)

    def pair_mine(p):
        mine = cot_t[:, core].reshape(ROWS, ROWS)
        dsum[p] = dot(mine, normed[x], 1, 0).reshape(NZ, PIECE, ROWS)

    def pair_end(p):
        copy_to(pair_stage.at[p], pair_recv.at[p], pair_send.at[p], pair_rsem.at[p], sibling).wait_recv()
        dsum[p] = dsum[p] + pair_recv[p].astype(F32)

    def ring_wait(p, i):
        copy_to(ring_stage.at[p, i], ring_recv.at[p, i], ring_send.at[p, i], ring_rsem.at[p, i], sibling).wait_recv()

    def ring_step(p, s):
        at = (z + step * (4 - s) + NZ) % NZ
        term = dsum[p, at]
        if s:
            ring_wait(p, s - 1)
            term = term + ring_recv[p, s - 1].astype(F32)
        ring_stage[p, s] = term.astype(BF16)
        send(ring_stage.at[p, s], ring_recv.at[p, s], ring_send.at[p, s], ring_rsem.at[p, s], d_major)
        if s < 3:
            at = (z - step * (3 - s) + NZ) % NZ
            term = dsum[p, at]
            if s:
                ring_wait(p, 3 + s)
                term = term + ring_recv[p, 3 + s].astype(F32)
            i = 4 + s
            ring_stage[p, i] = term.astype(BF16)
            send(ring_stage.at[p, i], ring_recv.at[p, i], ring_send.at[p, i], ring_rsem.at[p, i], d_minor)

    def ring_end(p):
        ring_wait(p, 3)
        ring_wait(p, 6)
        total = dsum[p, z] + ring_recv[p, 3].astype(F32) + ring_recv[p, 6].astype(F32)
        last_stage[p] = total.astype(BF16)
        a = quarters[p]

        @pl.when(a != y)
        def _():
            copy_to(last_stage.at[p], last_recv.at[y], last_send.at[p], last_rsem.at[y], dev(x, a, z, core)).start()

        @pl.when(a == y)
        def _():
            last_recv[y] = last_stage[p]

    quarters = (x, (x + 3) % NX, (x + 1) % NX, x_opp)

    def gn_part(p):
        w = wt[:, :, quarters[p]].reshape(NZ * 2 * PIECE, ROWS)
        part = dot(cot_of(p), w, 1, 0)
        gn[...] = part if p == 0 else gn[...] + part

    def gradient():
        for h in range(HEADS):
            w = gn[:, head(h)] * gain[:, head(h)]
            a = att[:, head(h)]
            along = jnp.mean(w * a, axis=-1, keepdims=True)
            ga[:, head(h)] = (inv[h] * (w - a * along)).astype(BF16)

    def queries_gradient(h):
        s = dot(ga[:, head(h)], v_ref[:, head(h)], 1, 1)
        m = jnp.where(row >= col, s, 0.0).astype(BF16)
        t = dot(m, k_ref[:, head(h)], 1, 0) + dot(ga[:, head(h)], state_of(0, h), 1, 1)
        gq_ref[:, head(h)] = t.astype(BF16)

    def local_keys_values(h):
        s = dot(v_ref[:, head(h)], ga[:, head(h)], 1, 1)
        m = jnp.where(col >= row, s, 0.0).astype(BF16)
        gn[:, head(h)] = dot(m, q_ref[:, head(h)], 1, 0)
        s = dot(k_ref[:, head(h)], q_ref[:, head(h)], 1, 1)
        m = jnp.where(col >= row, s, 0.0).astype(BF16)
        att[:, head(h)] = dot(m, ga[:, head(h)], 1, 0)

    def finish():
        for h in range(HEADS):
            st = state_of(1, h)
            gk_ref[:, head(h)] = (gn[:, head(h)] + dot(v_ref[:, head(h)], st, 1, 1)).astype(BF16)
            gv_ref[:, head(h)] = (att[:, head(h)] + dot(k_ref[:, head(h)], st, 1, 0)).astype(BF16)


    def out_part(p):
        a = quarters[p]
        part = dot(normed[a], wc[a].reshape(NZ * 2 * PIECE, ROWS), 1, 1)
        if p:
            part = part + acc[...]
        if p < NX - 1:
            acc[...] = part
        else:
            out_ref[...] = part.astype(BF16)

    def gw_sum():
        for d in range(1, NY):
            j = (y + d) % NY
            copy_to(last_stage.at[0], last_recv.at[j], last_send.at[0], last_rsem.at[j], sibling).wait_recv()
        gw_ref[...] = (
            (last_recv[0].astype(F32) + last_recv[1].astype(F32))
            + (last_recv[2].astype(F32) + last_recv[3].astype(F32))
        )

    for c in inputs[:2]:
        c.wait()
    scan_state(0)
    inputs[2].wait()
    local_attention(0)
    local_attention(1)
    local_attention(2)
    inputs[3].wait()

    @pl.when(x == y)
    def _():
        turn = pltpu.make_async_copy(w_ref, wc.at[x, z, core], in_sem.at[5])
        turn.start()
        turn.wait()

    pl.semaphore_wait(barrier, (GROUP - 1) + (NY - 1) + 3 - me_diag.astype(jnp.int32))

    @pl.when(x != y)
    def _():
        copy_to(w_ref, wc.at[x, z, core], pm_send.at[0], pm_recv.at[0], dev(y, x, z, core)).start()

    ring_cot[0].start(c_in.at[rows[0]])
    ring_bz.start()
    scan_start(0)
    ring_ay.start()
    local_attention(3)
    ring_cot[1].start(c_in.at[rows[1]])
    ring_bz.go(1)
    ring_ay.go(1)
    turned()
    ring_cz.start()
    scan_totals(0)
    ring_bz.go(2)
    ring_ay.go(2)
    ring_az.start()
    ring_cz.go(1)
    scan_back(0)
    ring_bz.go(3)
    ring_az.go(1)
    ring_cot[0].go(1)
    ring_cz.go(2)
    ring_bz.go(4)
    ring_by.start()
    scan_end(0)
    attend()
    ring_az.go(2)
    inputs[4].wait()
    pair_go(0)
    pair_mine(0)
    ring_cz.go(3)
    pair_end(0)
    ring_step(0, 0)
    ring_by.go(1)
    ring_az.go(3)
    ring_cot[1].go(1)
    pair_go(1)
    pair_mine(1)
    ring_cz.go(4)
    ring_cy.start()
    ring_step(0, 1)
    pair_end(1)
    ring_step(1, 0)
    ring_az.go(4)
    ring_by.go(2)
    exchanged(NZ, lambda i: az_view(i, 1 - core), ac_send, ac_recv)
    pair_go(2)
    ring_cot[0].go(2)
    exchanged(NY, lambda i: by_view(i, 1 - core), bc_send, bc_recv)
    ring_step(0, 2)
    gn_part(0)
    ring_step(1, 1)
    pair_mine(2)
    pair_end(2)
    ring_step(2, 0)
    gn_part(1)
    ring_n.start()
    gn_part(2)
    ring_step(0, 3)
    ring_cot[1].go(2)
    pair_go(3)
    ring_step(1, 2)
    gn_part(3)
    ring_step(2, 1)
    pair_mine(3)
    pair_end(3)
    ring_step(3, 0)
    gradient()
    ring_cy.go(1)
    scan_start(1)
    queries_gradient(0)
    queries_gradient(1)
    queries_gradient(2)
    ring_step(2, 2)
    local_keys_values(0)
    ring_step(3, 1)
    ring_end(0)
    ring_step(1, 3)
    local_keys_values(1)
    local_keys_values(2)
    local_keys_values(3)
    ring_step(2, 3)
    scan_totals(1)
    ring_n.go(1)
    ring_step(3, 2)
    ring_cy.go(2)
    queries_gradient(3)
    ring_end(2)
    exchanged(NY, lambda i: cy_view(i, 1 - core), cc_send, cc_recv)
    out_part(0)
    ring_step(3, 3)
    ring_end(1)
    scan_back(1)
    out_part(1)
    out_part(2)
    ring_end(3)
    ring_n.go(2)
    out_part(3)
    scan_end(1)
    finish()
    gw_sum()

    for c in sent:
        c.wait_send()

    @pl.when(x != y)
    def _():
        copy_to(w_ref, wc.at[x, z, core], pm_send.at[0], pm_recv.at[0], sibling).wait_send()

    for p in range(NX):
        @pl.when(quarters[p] != y)
        def _():
            copy_to(last_stage.at[p], last_recv.at[y], last_send.at[p], last_rsem.at[y], sibling).wait_send()

    def left(d, carry):
        for way in range(2):
            to = (g + d) % GROUP
            copy_to(state.at[way, to], slices.at[way, g], s1_send.at[way, d], s1_recv.at[way, g], sibling).wait_send()
            copy_to(back.at[way, to], states.at[way, g], s3_send.at[way, d], s3_recv.at[way, g], sibling).wait_send()
        return carry

    lax.fori_loop(1, GROUP, left, 0)


def settle(*refs):
    n = (len(refs) - 1) // 2
    copies = [pltpu.make_async_copy(refs[i], refs[n + i], refs[-1].at[i]) for i in range(n)]
    for c in copies:
        c.start()
    for c in copies:
        c.wait()


def on_device(queries, keys, values, gain, out_weight, cotangent):
    width = HEADS * HDIM
    cols = NZ * 2 * PIECE
    vmem = pl.BlockSpec(memory_space=pltpu.VMEM)
    anywhere = pl.BlockSpec(memory_space=pl.ANY)
    hbm = pl.BlockSpec(memory_space=pltpu.HBM)
    dma = pltpu.SemaphoreType.DMA
    outs = pl.pallas_call(
        kernel,
        out_shape=(
            pltpu.VMEM((ROWS, cols), BF16),
            pltpu.VMEM((ROWS, width), BF16),
            pltpu.VMEM((ROWS, width), BF16),
            pltpu.VMEM((ROWS, width), BF16),
            pltpu.VMEM((PIECE, width), F32),
        ),
        in_specs=[hbm, hbm, hbm, vmem, hbm, hbm],
        out_specs=(vmem,) * 5,
        scratch_shapes=[
            pltpu.VMEM((ROWS, width), BF16),
            pltpu.VMEM((ROWS, width), BF16),
            pltpu.VMEM((ROWS, width), BF16),
            pltpu.VMEM((ROWS, cols), BF16),
            pltpu.VMEM((NZ, 2, NY, PIECE, width), BF16),
            pltpu.VMEM((NX, NZ, 2, PIECE, width), BF16),
            pltpu.VMEM((NX, ROWS, cols), BF16),
            pltpu.VMEM((2, GROUP, SLICE, HDIM), BF16),
            pltpu.VMEM((2, GROUP, SLICE, HDIM), BF16),
            pltpu.VMEM((2, GROUP, SLICE, HDIM), F32),
            pltpu.VMEM((2, NY, SLICE, HDIM), F32),
            pltpu.VMEM((2, GROUP, SLICE, HDIM), BF16),
            pltpu.VMEM((2, GROUP, SLICE, HDIM), BF16),
            pltpu.VMEM((ROWS, width), F32),
            pltpu.VMEM((HEADS, ROWS, 1), F32),
            pltpu.VMEM((NX, ROWS, width), BF16),
            pltpu.VMEM((NZ, 2, PIECE, ROWS), BF16),
            pltpu.VMEM((ROWS, width), F32),
            pltpu.VMEM((ROWS, width), BF16),
            pltpu.VMEM((ROWS, cols), F32),
            pltpu.VMEM((NX, NZ, PIECE, width), BF16),
            pltpu.VMEM((NX, NZ, PIECE, width), BF16),
            pltpu.VMEM((NX, NZ, PIECE, width), F32),
            pltpu.VMEM((NX, 7, PIECE, width), BF16),
            pltpu.VMEM((NX, 7, PIECE, width), BF16),
            pltpu.VMEM((NX, PIECE, width), BF16),
            pltpu.VMEM((NY, PIECE, width), BF16),
            dma((6,)),
            dma((3,)), dma((3,)), dma((7,)), dma((7,)), dma((NZ,)), dma((NZ,)),
            dma((7,)), dma((7,)), dma((3,)), dma((3,)), dma((NY,)), dma((NY,)),
            dma((1,)), dma((1,)), dma((7,)), dma((7,)), dma((3,)), dma((3,)), dma((NY,)), dma((NY,)),
            dma((2, 3)), dma((2, 3)),
            dma((2, GROUP)), dma((2, GROUP)), dma((2, NY)), dma((2, NY)), dma((2, GROUP)), dma((2, GROUP)),
            dma((3,)), dma((3,)), dma((NX,)), dma((NX,)),
            dma((NX, 7)), dma((NX, 7)), dma((NX,)), dma((NY,)),
        ],
        compiler_params=pltpu.CompilerParams(
            collective_id=0, has_side_effects=True, vmem_limit_bytes=60 * 1024 * 1024
        ),
    )(queries, keys, values, gain, out_weight.T, cotangent)
    outs = [pltpu.with_memory_space_constraint(o, pltpu.VMEM) for o in outs]
    outs = pl.pallas_call(
        settle,
        out_shape=tuple(jax.ShapeDtypeStruct(o.shape, o.dtype) for o in outs),
        in_specs=[vmem] * len(outs),
        out_specs=(anywhere,) * len(outs),
        scratch_shapes=[dma((len(outs),))],
        compiler_params=pltpu.CompilerParams(vmem_limit_bytes=1024 * 1024),
    )(*outs)
    return outs[:4] + (outs[4].T,)


def solution(mesh):
    in_specs = (
        P("ctx", "head"),
        P("ctx", "head"),
        P("ctx", "head"),
        P("head"),
        P("head", "ctx"),
        P("ctx", "head"),
    )
    out_specs = (
        P("ctx", "head"),
        P("ctx", "head"),
        P("ctx", "head"),
        P("ctx", "head"),
        P("head", "ctx"),
    )
    return jax.shard_map(
        on_device, mesh=mesh, in_specs=in_specs, out_specs=out_specs, check_vma=False
    )
```

```python
import jax
import jax.numpy as jnp
from jax import lax
from jax.experimental import pallas as pl
from jax.experimental.pallas import tpu as pltpu
from jax.sharding import PartitionSpec as P

HDIM = 128
HEADS = 4
ROWS = 512
NX, NY, NZ = 4, 4, 8
GROUP = 2 * NZ
SLICE = HEADS * HDIM // GROUP
PIECE = 64
EPS = 1e-06
MESH = pl.DeviceIdType.MESH
F32, BF16 = jnp.float32, jnp.bfloat16


def dot(a, b, ca, cb):
    return lax.dot_general(a, b, (((ca,), (cb,)), ((), ())), preferred_element_type=F32)


def copy_to(src, dst, send_sem, recv_sem, device):
    return pltpu.make_async_remote_copy(
        src_ref=src, dst_ref=dst, send_sem=send_sem, recv_sem=recv_sem,
        device_id=device, device_id_type=MESH,
    )


def head(h):
    return slice(h * HDIM, (h + 1) * HDIM)


class Ring:
    def __init__(self, n, at, step, view, send_sem, recv_sem, device, sent, landed=None):
        self.n, self.at, self.step, self.view = n, at, step, view
        self.sems = send_sem, recv_sem
        self.major, self.minor = device((at + step + n) % n), device((at - step + n) % n)
        self.sent, self.landed = sent, landed

    def send(self, i, src, place, way):
        c = copy_to(src, self.view(place), self.sems[0].at[i], self.sems[1].at[i], way)
        c.start()
        self.sent.append(c)

    def arrive(self, i, place):
        view = self.view(place)
        copy_to(view, view, self.sems[0].at[i], self.sems[1].at[i], self.major).wait_recv()

    def start(self, src=None):
        src = self.view(self.at) if src is None else src
        self.send(0, src, self.at, self.major)
        self.send(self.n // 2, src, self.at, self.minor)
        if self.landed:
            self.landed(self.at)

    def go(self, s):
        n, half = self.n, self.n // 2
        places = [((self.at - self.step * s + n) % n, s - 1, s, self.major, s < half)]
        if s < half:
            places.append(((self.at + self.step * s + n) % n, half + s - 1, half + s, self.minor, s < half - 1))
        for place, came, goes, way, more in places:
            self.arrive(came, place)
            if more:
                self.send(goes, self.view(place), place, way)
            if self.landed:
                self.landed(place)


def kernel(
    q_in, k_in, v_in, g_ref, w_ref, c_in,
    out_ref, gq_ref, gk_ref, gv_ref, gw_ref,
    q_ref, k_ref, v_ref, c_ref, wt, wc, ca, state, slices, partial, totals, back, states,
    att, inv, normed, cot_t, gn, ga, acc,
    pair_stage, pair_recv, dsum, ring_stage, ring_recv, last_stage, last_recv,
    in_sem, ay_send, ay_recv, az_send, az_recv, ac_send, ac_recv,
    bz_send, bz_recv, by_send, by_recv, bc_send, bc_recv,
    pm_send, pm_recv, cz_send, cz_recv, cy_send, cy_recv, cc_send, cc_recv,
    ca_send, ca_recv,
    s1_send, s1_recv, s2_send, s2_recv, s3_send, s3_recv,
    n_send, n_recv, pair_send, pair_rsem,
    ring_send, ring_rsem, last_send, last_rsem,
):
    ctx, x = lax.axis_index("ctx"), lax.axis_index("head")
    y, z, core = ctx // GROUP, (ctx // 2) % NZ, ctx % 2
    g = ctx % GROUP
    me_diag = x == y

    def dev(x, y, z, core):
        return (y * GROUP + z * 2 + core, x)

    step = 1 - 2 * core
    z_major, z_minor = (z + step + NZ) % NZ, (z - step + NZ) % NZ
    x_opp = (x + 2) % NX
    d_major, d_minor = dev(x, y, z_major, core), dev(x, y, z_minor, core)
    sibling = dev(x, y, z, 1 - core)
    sent = []

    def send(*args):
        c = copy_to(*args)
        c.start()
        sent.append(c)

    barrier = pltpu.get_barrier_semaphore()

    def hello(device):
        pl.semaphore_signal(barrier, inc=1, device_id=device, device_id_type=MESH)

    def hello_group(d, carry):
        hello((y * GROUP + (g + d) % GROUP, x))
        return carry

    lax.fori_loop(1, GROUP, hello_group, 0)
    for d in range(1, NY):
        hello(dev(x, (y + d) % NY, z, core))
    hello(dev((x + 1) % NX, y, z, core))
    hello(dev((x + 3) % NX, y, z, core))

    @pl.when(x != y)
    def _():
        hello(dev(y, x, z, core))


    inputs = [
        pltpu.make_async_copy(there, here, in_sem.at[i])
        for i, (there, here) in enumerate(
            ((k_in, k_ref), (v_in, v_ref), (q_in, q_ref), (w_ref, wt.at[z, core, y]), (c_in, c_ref))
        )
    ]
    for c in inputs:
        c.start()

    def on_y(j):
        return dev(x, j, z, core)

    def on_z(j):
        return dev(x, y, j, core)

    def on_x(j):
        return dev(j, y, z, core)

    def exchange(view, send_sem, recv_sem):
        def landed(place):
            send(view(place), view(place), send_sem.at[place], recv_sem.at[place], sibling)

        return landed

    def exchanged(n, view, send_sem, recv_sem):
        for i in range(n):
            copy_to(view(i), view(i), send_sem.at[i], recv_sem.at[i], sibling).wait_recv()

    half = PIECE // 2
    low, high = pl.ds(0, half), pl.ds(half, half)
    az_view = lambda i, c=core: wt.at[i, c, :, low]
    by_view = lambda i, c=core: wt.at[:, c, i, high]
    cy_view = lambda i, c=core: wc.at[i, :, c]
    ring_ay = Ring(NY, y, step, lambda i: wt.at[z, core, i, low], ay_send, ay_recv, on_y, sent)
    ring_az = Ring(NZ, z, step, az_view, az_send, az_recv, on_z, sent, exchange(az_view, ac_send, ac_recv))
    ring_bz = Ring(NZ, z, step, lambda i: wt.at[i, core, y, high], bz_send, bz_recv, on_z, sent)
    ring_by = Ring(NY, y, step, by_view, by_send, by_recv, on_y, sent, exchange(by_view, bc_send, bc_recv))
    ring_cz = Ring(NZ, z, step, lambda i: wc.at[y, i, core], cz_send, cz_recv, on_z, sent)
    ring_cy = Ring(NY, y, step, cy_view, cy_send, cy_recv, on_y, sent, exchange(cy_view, cc_send, cc_recv))
    rows = [pl.ds(0, ROWS // 2), pl.ds(ROWS // 2, ROWS // 2)]
    ring_cot = [
        Ring(NX, x, step, lambda i, r=r: ca.at[i, r], ca_send.at[h], ca_recv.at[h], on_x, sent)
        for h, r in enumerate(rows)
    ]
    ring_n = Ring(NX, x, step, lambda i: normed.at[i], n_send, n_recv, on_x, sent)

    def turned():
        @pl.when(x != y)
        def _():
            copy_to(w_ref, wc.at[y, z, core], pm_send.at[0], pm_recv.at[0], sibling).wait_recv()

    def scan_state(way):
        for h in range(HEADS):
            state[way, h * (HDIM // SLICE):(h + 1) * (HDIM // SLICE)] = (
                scan_term(way, h).astype(BF16).reshape(HDIM // SLICE, SLICE, HDIM)
            )

    def scan_start(way):
        if way:
            scan_state(way)

        def go(d, carry):
            to = (g + d) % GROUP
            copy_to(state.at[way, to], slices.at[way, g], s1_send.at[way, d], s1_recv.at[way, g],
                    (y * GROUP + to, x)).start()
            return carry

        lax.fori_loop(1, GROUP, go, 0)
        slices[way, g] = state[way, g]

    def scan_term(way, h):
        if way == 0:
            return dot(k_ref[:, head(h)], v_ref[:, head(h)], 0, 0)
        return dot(q_ref[:, head(h)], ga[:, head(h)], 0, 0)

    def scan_totals(way):
        def arrive(d, carry):
            at = (g + d) % GROUP
            copy_to(slices.at[way, at], slices.at[way, at], s1_send.at[way, d], s1_recv.at[way, at], sibling).wait_recv()
            return carry

        lax.fori_loop(1, GROUP, arrive, 0)
        run = jnp.zeros((SLICE, HDIM), F32)
        for i in (range(GROUP) if way == 0 else range(GROUP - 1, -1, -1)):
            partial[way, i] = run
            run = run + slices[way, i].astype(F32)
        totals[way, y] = run
        for d in range(1, NY):
            send(totals.at[way, y], totals.at[way, y], s2_send.at[way, d], s2_recv.at[way, y],
                 dev(x, (y + d) % NY, z, core))

    def scan_back(way):
        for d in range(1, NY):
            at = (y + d) % NY
            copy_to(totals.at[way, at], totals.at[way, at], s2_send.at[way, d], s2_recv.at[way, at], sibling).wait_recv()
        offset = jnp.zeros((SLICE, HDIM), F32)
        for j in range(NY):
            counts = (j < y) if way == 0 else (j > y)
            offset = offset + jnp.where(counts, totals[way, j], 0.0)
        for i in range(GROUP):
            back[way, i] = (partial[way, i] + offset).astype(BF16)

        def go(d, carry):
            to = (g + d) % GROUP
            copy_to(back.at[way, to], states.at[way, g], s3_send.at[way, d], s3_recv.at[way, g],
                    (y * GROUP + to, x)).start()
            return carry

        lax.fori_loop(1, GROUP, go, 0)
        states[way, g] = back[way, g]

    def scan_end(way):
        def arrive(d, carry):
            at = (g + d) % GROUP
            copy_to(states.at[way, at], states.at[way, at], s3_send.at[way, d], s3_recv.at[way, at], sibling).wait_recv()
            return carry

        lax.fori_loop(1, GROUP, arrive, 0)

    def state_of(way, h):
        n = HDIM // SLICE
        return states[way, h * n:(h + 1) * n].reshape(HDIM, HDIM)


    gain = g_ref[...].astype(F32).reshape(1, HEADS * HDIM)
    row = lax.broadcasted_iota(jnp.int32, (ROWS, ROWS), 0)
    col = lax.broadcasted_iota(jnp.int32, (ROWS, ROWS), 1)

    def local_attention(h):
        s = dot(q_ref[:, head(h)], k_ref[:, head(h)], 1, 1)
        m = jnp.where(row >= col, s, 0.0).astype(BF16)
        att[:, head(h)] = dot(m, v_ref[:, head(h)], 1, 0)

    def attend():
        for h in range(HEADS):
            a = att[:, head(h)] + dot(q_ref[:, head(h)], state_of(0, h), 1, 0)
            scale = lax.rsqrt(jnp.mean(a * a, axis=-1, keepdims=True) + EPS)
            a = a * scale
            att[:, head(h)] = a
            inv[h] = scale
            normed[x, :, head(h)] = (a * gain[:, head(h)]).astype(BF16)


    def cot_of(p):
        return c_ref[...] if p == 0 else ca[quarters[p]]

    def pair_go(p):
        cot_t[...] = cot_of(p).T.reshape(NZ, 2, PIECE, ROWS)
        other = cot_t[:, 1 - core].reshape(ROWS, ROWS)
        pair_stage[p] = dot(other, normed[x], 1, 0).astype(BF16).reshape(NZ, PIECE, ROWS)
        send(pair_stage.at[p], pair_recv.at[p], pair_send.at[p], pair_rsem.at[p], sibling)

    def pair_mine(p):
        mine = cot_t[:, core].reshape(ROWS, ROWS)
        dsum[p] = dot(mine, normed[x], 1, 0).reshape(NZ, PIECE, ROWS)

    def pair_end(p):
        copy_to(pair_stage.at[p], pair_recv.at[p], pair_send.at[p], pair_rsem.at[p], sibling).wait_recv()
        dsum[p] = dsum[p] + pair_recv[p].astype(F32)

    def ring_wait(p, i):
        copy_to(ring_stage.at[p, i], ring_recv.at[p, i], ring_send.at[p, i], ring_rsem.at[p, i], sibling).wait_recv()

    def ring_step(p, s):
        at = (z + step * (4 - s) + NZ) % NZ
        term = dsum[p, at]
        if s:
            ring_wait(p, s - 1)
            term = term + ring_recv[p, s - 1].astype(F32)
        ring_stage[p, s] = term.astype(BF16)
        send(ring_stage.at[p, s], ring_recv.at[p, s], ring_send.at[p, s], ring_rsem.at[p, s], d_major)
        if s < 3:
            at = (z - step * (3 - s) + NZ) % NZ
            term = dsum[p, at]
            if s:
                ring_wait(p, 3 + s)
                term = term + ring_recv[p, 3 + s].astype(F32)
            i = 4 + s
            ring_stage[p, i] = term.astype(BF16)
            send(ring_stage.at[p, i], ring_recv.at[p, i], ring_send.at[p, i], ring_rsem.at[p, i], d_minor)

    def ring_end(p):
        ring_wait(p, 3)
        ring_wait(p, 6)
        total = dsum[p, z] + ring_recv[p, 3].astype(F32) + ring_recv[p, 6].astype(F32)
        last_stage[p] = total.astype(BF16)
        a = quarters[p]

        @pl.when(a != y)
        def _():
            copy_to(last_stage.at[p], last_recv.at[y], last_send.at[p], last_rsem.at[y], dev(x, a, z, core)).start()

        @pl.when(a == y)
        def _():
            last_recv[y] = last_stage[p]

    quarters = (x, (x + 3) % NX, (x + 1) % NX, x_opp)

    def gn_part(p):
        w = wt[:, :, quarters[p]].reshape(NZ * 2 * PIECE, ROWS)
        part = dot(cot_of(p), w, 1, 0)
        gn[...] = part if p == 0 else gn[...] + part

    def gradient():
        for h in range(HEADS):
            w = gn[:, head(h)] * gain[:, head(h)]
            a = att[:, head(h)]
            along = jnp.mean(w * a, axis=-1, keepdims=True)
            ga[:, head(h)] = (inv[h] * (w - a * along)).astype(BF16)

    def queries_gradient(h):
        s = dot(ga[:, head(h)], v_ref[:, head(h)], 1, 1)
        m = jnp.where(row >= col, s, 0.0).astype(BF16)
        t = dot(m, k_ref[:, head(h)], 1, 0) + dot(ga[:, head(h)], state_of(0, h), 1, 1)
        gq_ref[:, head(h)] = t.astype(BF16)

    def local_keys_values(h):
        s = dot(v_ref[:, head(h)], ga[:, head(h)], 1, 1)
        m = jnp.where(col >= row, s, 0.0).astype(BF16)
        gn[:, head(h)] = dot(m, q_ref[:, head(h)], 1, 0)
        s = dot(k_ref[:, head(h)], q_ref[:, head(h)], 1, 1)
        m = jnp.where(col >= row, s, 0.0).astype(BF16)
        att[:, head(h)] = dot(m, ga[:, head(h)], 1, 0)

    def finish():
        for h in range(HEADS):
            st = state_of(1, h)
            gk_ref[:, head(h)] = (gn[:, head(h)] + dot(v_ref[:, head(h)], st, 1, 1)).astype(BF16)
            gv_ref[:, head(h)] = (att[:, head(h)] + dot(k_ref[:, head(h)], st, 1, 0)).astype(BF16)


    def out_part(p):
        a = quarters[p]
        part = dot(normed[a], wc[a].reshape(NZ * 2 * PIECE, ROWS), 1, 1)
        if p:
            part = part + acc[...]
        if p < NX - 1:
            acc[...] = part
        else:
            out_ref[...] = part.astype(BF16)

    def gw_sum():
        for d in range(1, NY):
            j = (y + d) % NY
            copy_to(last_stage.at[0], last_recv.at[j], last_send.at[0], last_rsem.at[j], sibling).wait_recv()
        gw_ref[...] = (
            (last_recv[0].astype(F32) + last_recv[1].astype(F32))
            + (last_recv[2].astype(F32) + last_recv[3].astype(F32))
        )

    for c in inputs[:2]:
        c.wait()
    scan_state(0)
    inputs[2].wait()
    local_attention(0)
    local_attention(1)
    local_attention(2)
    local_attention(3)
    inputs[3].wait()

    @pl.when(x == y)
    def _():
        turn = pltpu.make_async_copy(w_ref, wc.at[x, z, core], in_sem.at[5])
        turn.start()
        turn.wait()

    pl.semaphore_wait(barrier, (GROUP - 1) + (NY - 1) + 3 - me_diag.astype(jnp.int32))

    @pl.when(x != y)
    def _():
        copy_to(w_ref, wc.at[x, z, core], pm_send.at[0], pm_recv.at[0], dev(y, x, z, core)).start()

    ring_cot[0].start(c_in.at[rows[0]])
    ring_bz.start()
    scan_start(0)
    ring_ay.start()
    ring_cot[1].start(c_in.at[rows[1]])
    ring_bz.go(1)
    ring_ay.go(1)
    turned()
    ring_cz.start()
    scan_totals(0)
    ring_bz.go(2)
    ring_ay.go(2)
    ring_az.start()
    ring_cz.go(1)
    scan_back(0)
    ring_bz.go(3)
    ring_az.go(1)
    ring_cot[0].go(1)
    ring_cz.go(2)
    ring_bz.go(4)
    ring_by.start()
    scan_end(0)
    attend()
    ring_az.go(2)
    inputs[4].wait()
    pair_go(0)
    pair_mine(0)
    ring_cz.go(3)
    pair_end(0)
    ring_step(0, 0)
    ring_by.go(1)
    ring_az.go(3)
    ring_cot[1].go(1)
    pair_go(1)
    pair_mine(1)
    ring_cz.go(4)
    ring_cy.start()
    ring_step(0, 1)
    pair_end(1)
    ring_step(1, 0)
    ring_az.go(4)
    ring_by.go(2)
    exchanged(NZ, lambda i: az_view(i, 1 - core), ac_send, ac_recv)
    pair_go(2)
    ring_cot[0].go(2)
    exchanged(NY, lambda i: by_view(i, 1 - core), bc_send, bc_recv)
    ring_step(0, 2)
    gn_part(0)
    ring_step(1, 1)
    pair_mine(2)
    pair_end(2)
    ring_step(2, 0)
    gn_part(1)
    ring_n.start()
    gn_part(2)
    ring_step(0, 3)
    ring_cot[1].go(2)
    pair_go(3)
    ring_step(1, 2)
    gn_part(3)
    ring_step(2, 1)
    pair_mine(3)
    pair_end(3)
    ring_step(3, 0)
    gradient()
    ring_cy.go(1)
    scan_start(1)
    queries_gradient(0)
    queries_gradient(1)
    queries_gradient(2)
    ring_step(2, 2)
    local_keys_values(0)
    ring_step(3, 1)
    ring_end(0)
    ring_step(1, 3)
    local_keys_values(1)
    local_keys_values(2)
    local_keys_values(3)
    ring_step(2, 3)
    scan_totals(1)
    ring_n.go(1)
    ring_step(3, 2)
    ring_cy.go(2)
    queries_gradient(3)
    ring_end(2)
    exchanged(NY, lambda i: cy_view(i, 1 - core), cc_send, cc_recv)
    out_part(0)
    ring_step(3, 3)
    ring_end(1)
    scan_back(1)
    out_part(1)
    out_part(2)
    ring_end(3)
    ring_n.go(2)
    out_part(3)
    scan_end(1)
    finish()
    gw_sum()

    for c in sent:
        c.wait_send()

    @pl.when(x != y)
    def _():
        copy_to(w_ref, wc.at[x, z, core], pm_send.at[0], pm_recv.at[0], sibling).wait_send()

    for p in range(NX):
        @pl.when(quarters[p] != y)
        def _():
            copy_to(last_stage.at[p], last_recv.at[y], last_send.at[p], last_rsem.at[y], sibling).wait_send()

    def left(d, carry):
        for way in range(2):
            to = (g + d) % GROUP
            copy_to(state.at[way, to], slices.at[way, g], s1_send.at[way, d], s1_recv.at[way, g], sibling).wait_send()
            copy_to(back.at[way, to], states.at[way, g], s3_send.at[way, d], s3_recv.at[way, g], sibling).wait_send()
        return carry

    lax.fori_loop(1, GROUP, left, 0)


def settle(*refs):
    n = (len(refs) - 1) // 2
    copies = [pltpu.make_async_copy(refs[i], refs[n + i], refs[-1].at[i]) for i in range(n)]
    for c in copies:
        c.start()
    for c in copies:
        c.wait()


def on_device(queries, keys, values, gain, out_weight, cotangent):
    width = HEADS * HDIM
    cols = NZ * 2 * PIECE
    vmem = pl.BlockSpec(memory_space=pltpu.VMEM)
    anywhere = pl.BlockSpec(memory_space=pl.ANY)
    hbm = pl.BlockSpec(memory_space=pltpu.HBM)
    dma = pltpu.SemaphoreType.DMA
    outs = pl.pallas_call(
        kernel,
        out_shape=(
            pltpu.VMEM((ROWS, cols), BF16),
            pltpu.VMEM((ROWS, width), BF16),
            pltpu.VMEM((ROWS, width), BF16),
            pltpu.VMEM((ROWS, width), BF16),
            pltpu.VMEM((PIECE, width), F32),
        ),
        in_specs=[hbm, hbm, hbm, vmem, hbm, hbm],
        out_specs=(vmem,) * 5,
        scratch_shapes=[
            pltpu.VMEM((ROWS, width), BF16),
            pltpu.VMEM((ROWS, width), BF16),
            pltpu.VMEM((ROWS, width), BF16),
            pltpu.VMEM((ROWS, cols), BF16),
            pltpu.VMEM((NZ, 2, NY, PIECE, width), BF16),
            pltpu.VMEM((NX, NZ, 2, PIECE, width), BF16),
            pltpu.VMEM((NX, ROWS, cols), BF16),
            pltpu.VMEM((2, GROUP, SLICE, HDIM), BF16),
            pltpu.VMEM((2, GROUP, SLICE, HDIM), BF16),
            pltpu.VMEM((2, GROUP, SLICE, HDIM), F32),
            pltpu.VMEM((2, NY, SLICE, HDIM), F32),
            pltpu.VMEM((2, GROUP, SLICE, HDIM), BF16),
            pltpu.VMEM((2, GROUP, SLICE, HDIM), BF16),
            pltpu.VMEM((ROWS, width), F32),
            pltpu.VMEM((HEADS, ROWS, 1), F32),
            pltpu.VMEM((NX, ROWS, width), BF16),
            pltpu.VMEM((NZ, 2, PIECE, ROWS), BF16),
            pltpu.VMEM((ROWS, width), F32),
            pltpu.VMEM((ROWS, width), BF16),
            pltpu.VMEM((ROWS, cols), F32),
            pltpu.VMEM((NX, NZ, PIECE, width), BF16),
            pltpu.VMEM((NX, NZ, PIECE, width), BF16),
            pltpu.VMEM((NX, NZ, PIECE, width), F32),
            pltpu.VMEM((NX, 7, PIECE, width), BF16),
            pltpu.VMEM((NX, 7, PIECE, width), BF16),
            pltpu.VMEM((NX, PIECE, width), BF16),
            pltpu.VMEM((NY, PIECE, width), BF16),
            dma((6,)),
            dma((3,)), dma((3,)), dma((7,)), dma((7,)), dma((NZ,)), dma((NZ,)),
            dma((7,)), dma((7,)), dma((3,)), dma((3,)), dma((NY,)), dma((NY,)),
            dma((1,)), dma((1,)), dma((7,)), dma((7,)), dma((3,)), dma((3,)), dma((NY,)), dma((NY,)),
            dma((2, 3)), dma((2, 3)),
            dma((2, GROUP)), dma((2, GROUP)), dma((2, NY)), dma((2, NY)), dma((2, GROUP)), dma((2, GROUP)),
            dma((3,)), dma((3,)), dma((NX,)), dma((NX,)),
            dma((NX, 7)), dma((NX, 7)), dma((NX,)), dma((NY,)),
        ],
        compiler_params=pltpu.CompilerParams(
            collective_id=0, has_side_effects=True, vmem_limit_bytes=60 * 1024 * 1024
        ),
    )(queries, keys, values, gain, out_weight.T, cotangent)
    outs = [pltpu.with_memory_space_constraint(o, pltpu.VMEM) for o in outs]
    outs = pl.pallas_call(
        settle,
        out_shape=tuple(jax.ShapeDtypeStruct(o.shape, o.dtype) for o in outs),
        in_specs=[vmem] * len(outs),
        out_specs=(anywhere,) * len(outs),
        scratch_shapes=[dma((len(outs),))],
        compiler_params=pltpu.CompilerParams(vmem_limit_bytes=1024 * 1024),
    )(*outs)
    return outs[:4] + (outs[4].T,)


def solution(mesh):
    in_specs = (
        P("ctx", "head"),
        P("ctx", "head"),
        P("ctx", "head"),
        P("head"),
        P("head", "ctx"),
        P("ctx", "head"),
    )
    out_specs = (
        P("ctx", "head"),
        P("ctx", "head"),
        P("ctx", "head"),
        P("ctx", "head"),
        P("head", "ctx"),
    )
    return jax.shard_map(
        on_device, mesh=mesh, in_specs=in_specs, out_specs=out_specs, check_vma=False
    )
```
